32 devices in a mesh: wide: 32 (over z, y, x, core), narrow: 1.
Axes of the slice: x: 2, y: 2, z: 4, core: 2. Of those that a mesh axis runs over, the one named last changes fastest.
Arguments:
- integrals: bfloat16 [2048, 128, 128], P('narrow', 'wide'), may hold values from -6 to 6
- fitted: bfloat16 [2048, 128, 128], P('narrow', 'wide'), may hold values from -0.00390625 to 0.00390625
- occupied: bfloat16 [128, 1024], P('wide'), may hold values from -0.5 to 0.5
- pattern: int32 [8, 8], replicated, may hold values 0 or 1
Outputs:
- exchange_matrix: float32 [128, 128], P('wide')
The draws below stay inside these ranges and needn't reach their ends.
All inputs are finite; a program needn't handle non-finite values.
Results may differ from the reference program's by a relative error of at most 0.0018.
Values may be sent and summed in bfloat16 or wider, within the bound.
No kernel may reach another device: no remote copies, remote signals or barrier semaphores. Data moves between devices by JAX's collectives and lax.ppermute only.
A program may use at most 64 MiB of HBM per device.

```python
import jax
import jax.numpy as jnp
from jax import lax

Q = 2048
OCC = 1024
NBLK = 8
NB = 128


def set_ends(entries, stream_key, low, largest):
    extent = entries.shape
    spot = [jax.random.randint(jax.random.fold_in(stream_key, axis), (), 0, extent[axis]) for axis in range(len(extent))]
    entries = entries.at[tuple(spot)].set(low)
    longest = extent.index(max(extent))
    spot[longest] = (spot[longest] + 1) % extent[longest]
    return entries.at[tuple(spot)].set(largest)


def block_levels(stream_key, extent, pieces, least, top_value):
    loudness = 1.0
    for dim, parts in pieces:
        heights = jax.random.uniform(jax.random.fold_in(jax.random.fold_in(stream_key, 6), dim), (parts,), jnp.float32, least / len(pieces), top_value / len(pieces))
        loudness = loudness * jnp.repeat(jnp.exp(heights), extent[dim] // parts).reshape((-1,) + (1,) * (len(extent) - 1 - dim))
    return loudness


def normal_values(key, shape, width, most, pieces=(), kind=jnp.bfloat16):
    entries = jax.random.normal(key, shape, jnp.float32) * width
    if len(pieces) > 0:
        entries = block_levels(key, shape, pieces, -0.22, 0.18) * entries
    return jnp.clip(entries, min=-most, max=most).astype(kind)


def setup_inputs(seed: int = 0) -> dict:
    keys = jax.random.split(jax.random.key(seed), 5)
    return {
        "integrals": normal_values(keys[0], (Q, NB, NB), 1.0, 6.0, ((1, 32),)),
        "fitted": normal_values(keys[1], (Q, NB, NB), (Q * OCC) ** -0.5, 0.00390625, ((1, 32),)),
        "occupied": normal_values(keys[2], (NB, OCC), NB ** -0.5, 0.5, ((0, 32),)),
        "pattern": set_ends((jax.random.randint(keys[3], (NBLK, NBLK), 0, 2) < 1).astype(jnp.int32), jax.random.fold_in(keys[3], 1), 0, 1),
    }


def reference(integrals, fitted, occupied, pattern):
    basis = integrals.shape[1]
    block_width = basis // NBLK
    block_ids = jnp.arange(basis) // block_width
    live = pattern[block_ids[:, None], block_ids[None, :]]
    live_mask = live.astype(jnp.float32)
    full_panel = occupied.astype(jnp.float32)
    aux_step = min(64, Q)
    ints_blocks = integrals.reshape(Q // aux_step, aux_step, basis, basis)
    fitted_blocks = fitted.reshape(Q // aux_step, aux_step, basis, basis)

    def accumulate(carry, blocks_pair):
        ints_part, fitted_part = blocks_pair
        half_ints = jnp.einsum("qml,li->qmi", ints_part.astype(jnp.float32) * live_mask, full_panel,
                               precision=lax.Precision.HIGHEST).astype(jnp.bfloat16)
        half_fitted = jnp.einsum("qml,li->qmi", fitted_part.astype(jnp.float32) * live_mask, full_panel,
                                 precision=lax.Precision.HIGHEST).astype(jnp.bfloat16)
        carry = carry + jnp.einsum("qmi,qni->mn", half_ints.astype(jnp.float32), half_fitted.astype(jnp.float32),
                                   precision=lax.Precision.HIGHEST)
        return carry, None

    partial_value, _ = lax.scan(accumulate, jnp.zeros((basis, basis), jnp.float32), (ints_blocks, fitted_blocks))
    return partial_value + partial_value.T
```

```python
import functools

import jax
import jax.numpy as jnp
import numpy as np
from jax import lax
from jax.experimental import pallas as pl
from jax.experimental.pallas import tpu as pltpu
from jax.sharding import PartitionSpec as P

NBLK = 8
FULL = NBLK // 2
VMEM_BYTES = 48 * 2**20


def parts_of(cap, groups):
    parts = []
    for piece in (FULL, FULL, FULL // 2, FULL // 4):
        if cap >= piece and FULL // piece <= groups:
            parts.append(piece)
            cap -= piece
    return parts if cap == 0 else None


def lane_codes(live, parts, groups, basis):
    width = basis // NBLK
    lane = np.arange(basis)
    slot, base, owner, offset = [], [], [], 0
    for piece in parts:
        shared = FULL // piece
        inner = lane % (basis // shared)
        slot.append(offset + inner % (piece * width) // width)
        base.append(inner // (piece * width) * basis + inner % width)
        owner.append(np.arange(groups)[:, None] * shared // groups == lane[None, :] // (basis // shared))
        offset += piece
    slot, base, owner = np.concatenate(slot), np.concatenate(base), np.concatenate(owner, axis=1)
    before = np.arange(NBLK)[:, None] < np.arange(NBLK)[None, :]
    rank = jnp.sum(live[:, :, None] * before[None].astype(np.int32), axis=1)
    here = (live[:, None, :] > 0) & (rank[:, None, :] == slot[None, :, None])
    column = base[None, :, None] + np.arange(NBLK)[None, None, :] * width + 1
    codes = jnp.sum(jnp.where(here, column.astype(np.int32), 0), axis=2) - 1
    return jnp.where(owner[None], codes[:, None, :], -1)


def one_hot(codes, height):
    rows = lax.broadcasted_iota(jnp.int32, (height, codes.shape[1]), 0)
    return jnp.where(rows == codes, 1.0, 0.0).astype(jnp.bfloat16)


def pack_kernel(parts, groups, codes_ref, ints_ref, fitted_ref, out_ref):
    chunks, rows, basis = ints_ref.shape
    step = rows // groups
    packed = []
    for group in range(groups):
        span = pl.ds(group * step, step)
        both = jnp.concatenate(
            [ints_ref[:, span, :].reshape(chunks * step, basis), fitted_ref[:, span, :].reshape(chunks * step, basis)],
            axis=1,
        )
        table = one_hot(codes_ref[group : group + 1, :], 2 * basis)
        packed.append(jnp.dot(both, table, preferred_element_type=jnp.float32))
    start = 0
    for index, piece in enumerate(parts):
        shared = FULL // piece
        for inner in range(groups // shared):
            lanes = slice(index * basis, (index + 1) * basis)
            total = packed[inner][:, lanes]
            for other in range(1, shared):
                total = total + packed[other * (groups // shared) + inner][:, lanes]
            out_ref[:, pl.ds(start, step), :] = total.astype(jnp.bfloat16).reshape(chunks, step, basis)
            start += step


def pack(ints, fitted, codes, parts, groups):
    count, rows, basis = ints.shape
    out_rows = sum(rows * piece // FULL for piece in parts)
    chunks = max(1, count // 4)
    block = pl.BlockSpec((chunks, rows, basis), lambda i: (i, 0, 0))
    return pl.pallas_call(
        functools.partial(pack_kernel, parts, groups),
        grid=(count // chunks,),
        out_shape=jax.ShapeDtypeStruct((count, out_rows, basis), jnp.bfloat16),
        in_specs=[pl.BlockSpec(codes.shape, lambda i: (0, 0)), block, block],
        out_specs=pl.BlockSpec((chunks, out_rows, basis), lambda i: (i, 0, 0)),
        compiler_params=pltpu.CompilerParams(vmem_limit_bytes=VMEM_BYTES),
        name="pack",
    )(codes, ints, fitted)


def contract_kernel(parts, groups, height, codes_ref, panel_ref, got_ref, out_ref, gram, left, right):
    sources, _, basis = got_ref.shape
    block = pl.program_id(0)
    step = height // groups

    @pl.when(block == 0)
    def _():
        panel = panel_ref[...]
        full = lax.dot_general(panel, panel, (((1,), (1,)), ((), ())), preferred_element_type=jnp.float32)
        high = full.astype(jnp.bfloat16)
        gram[:, :basis] = high
        gram[:, basis:] = (full - high.astype(jnp.float32)).astype(jnp.bfloat16)

    for group in range(groups):
        pieces, start = [], 0
        for piece in parts:
            kept = groups * piece // FULL
            span = pl.ds(start + group % kept * step, step)
            pieces.append(got_ref[:, span, :].reshape(sources * step, basis))
            start += kept * step
        packed = pieces[0] if len(pieces) == 1 else jnp.concatenate(pieces, axis=1)
        table = one_hot(codes_ref[0, group : group + 1, :], 2 * basis)
        both = lax.dot_general(packed, table, (((1,), (1,)), ((), ())), preferred_element_type=jnp.float32)
        ints = both[:, :basis].astype(jnp.bfloat16)
        turned = jnp.dot(ints, gram[...], preferred_element_type=jnp.float32)
        turned = (turned[:, :basis] + turned[:, basis:]).reshape(sources, step, basis)
        fitted = both[:, basis:].reshape(sources, step, basis)
        rows = pl.ds(pl.multiple_of(block * (sources * 8), sources * 8), sources * 8)
        for eight in range(step // 8):
            at = (group * (step // 8) + eight) * 2 * basis
            mine = turned[:, eight * 8 : eight * 8 + 8, :].reshape(sources * 8, basis)
            high = mine.astype(jnp.bfloat16)
            left[rows, at : at + basis] = high
            left[rows, at + basis : at + 2 * basis] = (mine - high.astype(jnp.float32)).astype(jnp.bfloat16)
            theirs = fitted[:, eight * 8 : eight * 8 + 8, :].reshape(sources * 8, basis).astype(jnp.bfloat16)
            right[rows, at : at + basis] = theirs
            right[rows, at + basis : at + 2 * basis] = theirs

    @pl.when(block == pl.num_programs(0) - 1)
    def _():
        wide, per = left.shape[0], out_ref.shape[0] * 8 // left.shape[0]
        total = lax.dot_general(
            left[...], right[...], (((1,), (1,)), ((), ())), preferred_element_type=jnp.float32
        )
        row = lax.broadcasted_iota(jnp.int32, (wide, wide), 0) % 8 // per
        column = lax.broadcasted_iota(jnp.int32, (wide, wide), 1) % 8 // per
        total = jnp.where(row == column, total, 0.0)
        total = total + total.T
        spot = lax.broadcasted_iota(jnp.int32, (basis, wide), 1)
        spot = spot // 8 * per + spot % per
        fold = jnp.where(spot == lax.broadcasted_iota(jnp.int32, (basis, wide), 0), 1.0, 0.0)
        total = jnp.dot(fold, total, precision=lax.Precision.HIGHEST, preferred_element_type=jnp.float32)
        out_ref[...] = lax.dot_general(
            total,
            fold,
            (((1,), (1,)), ((), ())),
            precision=lax.Precision.HIGHEST,
            preferred_element_type=jnp.float32,
        )


def contract(got, codes, panel, parts, groups, height):
    count, rows, basis = got.shape
    sources = count // NBLK
    depth = height // 8 * 2 * basis
    return pl.pallas_call(
        functools.partial(contract_kernel, parts, groups, height),
        grid=(NBLK,),
        out_shape=jax.ShapeDtypeStruct((basis, basis), jnp.float32),
        in_specs=[
            pl.BlockSpec((1,) + codes.shape[1:], lambda i: (i, 0, 0)),
            pl.BlockSpec(panel.shape, lambda i: (0, 0)),
            pl.BlockSpec((sources, rows, basis), lambda i: (i, 0, 0)),
        ],
        out_specs=pl.BlockSpec((basis, basis), lambda i: (0, 0)),
        scratch_shapes=[
            pltpu.VMEM((basis, 2 * basis), jnp.bfloat16),
            pltpu.VMEM((count * 8, depth), jnp.bfloat16),
            pltpu.VMEM((count * 8, depth), jnp.bfloat16),
        ],
        compiler_params=pltpu.CompilerParams(vmem_limit_bytes=VMEM_BYTES),
        name="contract",
    )(codes, panel, got)


def gather_panel(occupied, count):
    if count & (count - 1):
        return lax.all_gather(occupied, "wide", axis=0, tiled=True)
    me, bit, rows = lax.axis_index("wide"), 1, occupied
    while bit < count:
        other = lax.ppermute(rows, "wide", [(i, i ^ bit) for i in range(count)])
        low = me // bit % 2 == 0
        rows = jnp.where(low, jnp.concatenate([rows, other]), jnp.concatenate([other, rows]))
        bit *= 2
    return rows


def share(parts, groups, count, integrals, fitted, occupied, live):
    aux, per, basis = integrals.shape
    height = aux // count * per
    codes = lane_codes(live, parts, groups, basis)
    mine = lax.dynamic_index_in_dim(codes, lax.axis_index("wide") * NBLK // count, 0, False)
    packed = pack(
        integrals.reshape(count, height, basis), fitted.reshape(count, height, basis), mine, parts, groups
    )
    got = lax.all_to_all(packed, "wide", split_axis=0, concat_axis=0, tiled=True)
    panel = gather_panel(occupied, count)
    return contract(got, codes, panel, parts, groups, height)


def on_device(count, narrow, integrals, fitted, occupied, pattern):
    aux, per, basis = integrals.shape
    groups = next(g for g in (FULL, FULL // 2, 1) if aux // count * per % (16 * g) == 0)
    choices = [(cap, parts_of(cap, groups)) for cap in range(1, NBLK + 1)]
    choices = [(cap, parts) for cap, parts in choices if parts is not None]
    live = (pattern != 0).astype(jnp.int32)
    most = jnp.max(jnp.sum(live, axis=1))
    choice = sum((most > cap).astype(jnp.int32) for cap, _ in choices[:-1])
    branches = [functools.partial(share, parts, groups, count) for _, parts in choices]
    total = lax.switch(choice, branches, integrals, fitted, occupied, live)
    strips = lax.all_to_all(total.reshape(count, per, basis), "wide", split_axis=0, concat_axis=0, tiled=True)
    strip = jnp.sum(strips.reshape(count, per, basis), axis=0)
    return lax.psum(strip, "narrow") if narrow > 1 else strip


def solution(mesh):
    in_specs = (P("narrow", "wide", None), P("narrow", "wide", None), P("wide", None), P())
    out_specs = P("wide", None)
    body = functools.partial(on_device, mesh.shape["wide"], mesh.shape["narrow"])
    return jax.shard_map(body, mesh=mesh, in_specs=in_specs, out_specs=out_specs, check_vma=False)
```

```python
import functools

import jax
import jax.numpy as jnp
import numpy as np
from jax import lax
from jax.experimental import pallas as pl
from jax.experimental.pallas import tpu as pltpu
from jax.sharding import PartitionSpec as P

NBLK = 8
FULL = NBLK // 2
PACK_STEPS = 4
DEPTH = 512
VMEM = 62 * 2**20
NT = (((1,), (1,)), ((), ()))


def parts_of(cap, groups):
    parts = []
    for piece in (FULL, FULL, FULL // 2, FULL // 4):
        if cap >= piece and FULL // piece <= groups:
            parts.append(piece)
            cap -= piece
    return parts if cap == 0 else None


def lane_layout(parts, basis):
    width = basis // NBLK
    lane = np.arange(basis)
    slot, base, offset = [], [], 0
    for piece in parts:
        inner = lane % (basis * piece // FULL)
        slot.append(offset + inner % (piece * width) // width)
        base.append(inner // (piece * width) * basis + inner % width)
        offset += piece
    return np.stack([np.concatenate(slot), np.concatenate(base)]).astype(np.int32)


def columns_of(pattern_ref, block, slot, base, width):
    columns = jnp.full(slot.shape, -1, jnp.int32)
    rank = jnp.int32(0)
    for other in range(NBLK):
        alive = pattern_ref[block, other] != 0
        columns = jnp.where(slot == jnp.where(alive, rank, -1), base + other * width, columns)
        rank = rank + alive.astype(jnp.int32)
    return columns


def halves(wide):
    high = wide.astype(jnp.bfloat16)
    return high, (wide - high.astype(jnp.float32)).astype(jnp.bfloat16)


def pack_kernel(parts, groups, block_ref, pattern_ref, layout_ref, ints_hbm, fitted_hbm, out_hbm, both, out, table, in_sems, out_sems):
    count, rows, lanes = both.shape
    basis = lanes // 2
    steps = in_sems.shape[0]
    chunks = count // steps
    step = rows // groups

    def arrivals(turn):
        here = pl.ds(turn * chunks, chunks)
        return (
            pltpu.make_async_copy(ints_hbm.at[here], both.at[here, :, pl.ds(0, basis)], in_sems.at[turn, 0]),
            pltpu.make_async_copy(fitted_hbm.at[here], both.at[here, :, pl.ds(basis, basis)], in_sems.at[turn, 1]),
        )

    def departure(turn):
        here = pl.ds(turn * chunks, chunks)
        return pltpu.make_async_copy(out.at[here], out_hbm.at[here], out_sems.at[turn])

    for turn in range(steps):
        for copy in arrivals(turn):
            copy.start()

    layout = layout_ref[...]
    columns = columns_of(pattern_ref, block_ref[0], layout[0:1], layout[1:2], basis // NBLK)
    height = lax.broadcasted_iota(jnp.int32, table.shape, 0)
    table[...] = jnp.where(height == columns, 1.0, 0.0).astype(jnp.bfloat16)

    lane = lax.broadcasted_iota(jnp.int32, (chunks * step, basis), 1)

    def work(turn, _):
        for copy in arrivals(turn):
            copy.wait()
        here = pl.ds(turn * chunks, chunks)
        packed = []
        for group in range(groups):
            mine = both[here, pl.ds(group * step, step), :].reshape(chunks * step, lanes)
            packed.append(jnp.dot(mine, table[...], preferred_element_type=jnp.float32))
        start = 0
        for index, piece in enumerate(parts):
            shared = FULL // piece
            held = slice(index * basis, (index + 1) * basis)
            for inner in range(groups // shared):
                total = packed[inner][:, held]
                for other in range(1, shared):
                    theirs = packed[other * (groups // shared) + inner][:, held]
                    total = jnp.where(lane >= other * (basis // shared), theirs, total)
                out[here, pl.ds(start, step), :] = total.astype(jnp.bfloat16).reshape(chunks, step, basis)
                start += step
        departure(turn).start()
        return 0

    lax.fori_loop(0, steps, work, 0)
    for turn in range(steps):
        departure(turn).wait()


def pack(ints, fitted, block, pattern, parts, groups):
    count, rows, basis = ints.shape
    out_rows = sum(rows * piece // FULL for piece in parts)
    steps = PACK_STEPS if count % PACK_STEPS == 0 else 1
    layout = lane_layout(parts, basis)
    flops = 2 * count * rows * 2 * basis * layout.shape[1]
    moved = 2 * ints.nbytes + 2 * count * out_rows * basis
    return pl.pallas_call(
        functools.partial(pack_kernel, parts, groups),
        out_shape=jax.ShapeDtypeStruct((count, out_rows, basis), jnp.bfloat16),
        in_specs=[
            pl.BlockSpec(memory_space=pltpu.SMEM),
            pl.BlockSpec(memory_space=pltpu.SMEM),
            pl.BlockSpec(memory_space=pltpu.VMEM),
            pl.BlockSpec(memory_space=pl.ANY),
            pl.BlockSpec(memory_space=pl.ANY),
        ],
        out_specs=pl.BlockSpec(memory_space=pl.ANY),
        scratch_shapes=[
            pltpu.VMEM((count, rows, 2 * basis), jnp.bfloat16),
            pltpu.VMEM((count, out_rows, basis), jnp.bfloat16),
            pltpu.VMEM((2 * basis, layout.shape[1]), jnp.bfloat16),
            pltpu.SemaphoreType.DMA((steps, 2)),
            pltpu.SemaphoreType.DMA((steps,)),
        ],
        compiler_params=pltpu.CompilerParams(vmem_limit_bytes=VMEM),
        cost_estimate=pl.CostEstimate(flops=flops, bytes_accessed=moved, transcendentals=0),
        name="pack",
    )(block, pattern, jnp.asarray(layout), ints, fitted)


def weights_kernel(pattern_ref, layout_ref, panel_ref, out_ref):
    basis = panel_ref.shape[0]
    lanes = layout_ref.shape[0]
    panel = panel_ref[...]
    gram = lax.dot_general(panel, panel, NT, preferred_element_type=jnp.float32)
    high, low = halves(gram)
    column = lax.broadcasted_iota(jnp.int32, (lanes, 2 * basis), 1)

    def fill(block, _):
        held = columns_of(pattern_ref, block, layout_ref[:, 0:1], layout_ref[:, 1:2], basis // NBLK)
        table = jnp.where(column == held, 1.0, 0.0).astype(jnp.bfloat16)
        ints = table[:, :basis]
        out_ref[block, :lanes, :basis] = jnp.dot(ints, high, preferred_element_type=jnp.float32).astype(jnp.bfloat16)
        out_ref[block, :lanes, basis:] = table[:, basis:]
        out_ref[block, lanes:, :basis] = jnp.dot(ints, low, preferred_element_type=jnp.float32).astype(jnp.bfloat16)
        out_ref[block, lanes:, basis:] = jnp.zeros((lanes, basis), jnp.bfloat16)
        return 0

    lax.fori_loop(0, NBLK, fill, 0)


def weights(panel, pattern, parts):
    basis = panel.shape[0]
    layout = lane_layout(parts, basis).T
    lanes = layout.shape[0]
    return pl.pallas_call(
        weights_kernel,
        out_shape=jax.ShapeDtypeStruct((NBLK, 2 * lanes, 2 * basis), jnp.bfloat16),
        in_specs=[
            pl.BlockSpec(memory_space=pltpu.SMEM),
            pl.BlockSpec(memory_space=pltpu.VMEM),
            pl.BlockSpec(memory_space=pltpu.VMEM),
        ],
        out_specs=pl.BlockSpec(memory_space=pltpu.VMEM),
        compiler_params=pltpu.CompilerParams(vmem_limit_bytes=VMEM),
        cost_estimate=pl.CostEstimate(flops=2 * NBLK * 2 * lanes * basis * basis, bytes_accessed=2 * panel.nbytes, transcendentals=0),
        name="weights",
    )(pattern, jnp.asarray(layout), panel)


def contract_kernel(parts, groups, per, tables_hbm, got_hbm, out_ref, tables, got, left, right, sems):
    count, _, basis = got.shape
    sources = count // NBLK
    height = right.shape[1] // basis * 8
    step = height // groups
    wide = count * 8

    def arrivals(block):
        here = pl.ds(block * sources, sources)
        return (
            pltpu.make_async_copy(tables_hbm.at[block], tables.at[block], sems.at[block, 0]),
            pltpu.make_async_copy(got_hbm.at[here], got.at[here], sems.at[block, 1]),
        )

    for block in range(NBLK):
        for copy in arrivals(block):
            copy.start()

    def unpack(block, _):
        for copy in arrivals(block):
            copy.wait()
        here = pl.ds(block * sources, sources)
        pieces, start = [], 0
        for piece in parts:
            shared = FULL // piece
            kept = groups // shared * step
            part = got[here, pl.ds(start, kept), :]
            start += kept
            if shared > 1:
                lane = lax.broadcasted_iota(jnp.int32, part.shape, 2)
                window = basis // shared
                part = jnp.concatenate(
                    [
                        jnp.where((lane >= own * window) & (lane < (own + 1) * window), part, jnp.zeros_like(part))
                        for own in range(shared)
                    ],
                    axis=1,
                )
            pieces.append(part.reshape(sources * height, basis))
        both = jnp.concatenate(pieces + pieces, axis=1)
        turned = jnp.dot(both, tables[block], preferred_element_type=jnp.float32).reshape(sources, height, 2 * basis)
        rows = pl.ds(pl.multiple_of(block * (sources * 8), sources * 8), sources * 8)
        low_rows = pl.ds(pl.multiple_of(block * (sources * 8) + wide, sources * 8), sources * 8)
        for eight in range(height // 8):
            lanes = slice(eight * basis, (eight + 1) * basis)
            mine = turned[:, eight * 8 : eight * 8 + 8, :].reshape(sources * 8, 2 * basis)
            high = mine[:, :basis].astype(jnp.bfloat16)
            left[rows, lanes] = high
            left[low_rows, lanes] = (mine[:, :basis] - high.astype(jnp.float32)).astype(jnp.bfloat16)
            right[rows, lanes] = mine[:, basis:].astype(jnp.bfloat16)
        return 0

    lax.fori_loop(0, NBLK, unpack, 0)
    turns = right.shape[1] // DEPTH if right.shape[1] % DEPTH == 0 else 1
    depth = right.shape[1] // turns

    def multiply(turn, sums):
        lanes = pl.ds(pl.multiple_of(turn * depth, depth), depth)
        return sums + lax.dot_general(left[:, lanes], right[:, lanes], NT, preferred_element_type=jnp.float32)

    total = lax.fori_loop(0, turns, multiply, jnp.zeros((2 * wide, wide), jnp.float32))
    total = total[:wide] + total[wide:]
    row = lax.broadcasted_iota(jnp.int32, (wide, wide), 0) % 8 // per
    column = lax.broadcasted_iota(jnp.int32, (wide, wide), 1) % 8 // per
    total = jnp.where(row == column, total, 0.0)
    spot = lax.broadcasted_iota(jnp.int32, (basis, wide), 1)
    spot = spot // 8 * per + spot % per
    fold = jnp.where(spot == lax.broadcasted_iota(jnp.int32, (basis, wide), 0), 1.0, 0.0).astype(jnp.bfloat16)
    high, low = halves(total)
    total = jnp.dot(fold, high, preferred_element_type=jnp.float32) + jnp.dot(
        fold, low, preferred_element_type=jnp.float32
    )
    high, low = halves(total)
    total = lax.dot_general(high, fold, NT, preferred_element_type=jnp.float32) + lax.dot_general(
        low, fold, NT, preferred_element_type=jnp.float32
    )
    out_ref[...] = total + total.T


def contract(got, tables, parts, groups, height, per):
    count, _, basis = got.shape
    deep = height // 8 * basis
    return pl.pallas_call(
        functools.partial(contract_kernel, parts, groups, per),
        out_shape=jax.ShapeDtypeStruct((basis, basis), jnp.float32),
        in_specs=[pl.BlockSpec(memory_space=pl.ANY)] * 2,
        out_specs=pl.BlockSpec(memory_space=pltpu.VMEM),
        scratch_shapes=[
            pltpu.VMEM(tables.shape, jnp.bfloat16),
            pltpu.VMEM(got.shape, jnp.bfloat16),
            pltpu.VMEM((count * 16, deep), jnp.bfloat16),
            pltpu.VMEM((count * 8, deep), jnp.bfloat16),
            pltpu.SemaphoreType.DMA((NBLK, 2)),
        ],
        compiler_params=pltpu.CompilerParams(vmem_limit_bytes=VMEM),
        name="contract",
    )(tables, got)


def widen(rows, bits, count):
    me, size = lax.axis_index("wide"), 2 ** len(bits)
    masks = [sum(bit for place, bit in enumerate(reversed(bits)) if turn >> place & 1) for turn in range(size)]
    got = [rows] + [lax.ppermute(rows, "wide", [(i, i ^ mask) for i in range(count)]) for mask in masks[1:]]
    for place, bit in enumerate(reversed(bits)):
        low = me // bit % 2 == 0
        got = [jnp.where(low, got[turn], got[turn ^ 1 << place]) for turn in range(size)]
    return jnp.stack(got, axis=1).reshape((-1,) + rows.shape[1:])


def choose(pattern, caps):
    def kernel(pattern_ref, out_ref):
        most = jnp.int32(0)
        for block in range(NBLK):
            alive = jnp.int32(0)
            for other in range(NBLK):
                alive = alive + (pattern_ref[block, other] != 0).astype(jnp.int32)
            most = jnp.maximum(most, alive)
        choice = jnp.int32(0)
        for cap in caps:
            choice = choice + (most > cap).astype(jnp.int32)
        out_ref[0] = choice

    return pl.pallas_call(
        kernel,
        out_shape=jax.ShapeDtypeStruct((1,), jnp.int32),
        in_specs=[pl.BlockSpec(memory_space=pltpu.SMEM)],
        out_specs=pl.BlockSpec(memory_space=pltpu.SMEM),
        name="choose",
    )(pattern)[0]


def share(parts, groups, count, integrals, fitted, occupied, pattern):
    aux, per, basis = integrals.shape
    height = aux // count * per
    block = (lax.axis_index("wide") * NBLK // count).astype(jnp.int32).reshape(1)
    packed = pack(
        integrals.reshape(count, height, basis), fitted.reshape(count, height, basis), block, pattern, parts, groups
    )
    panel = occupied[None]
    bits = [1 << place for place in reversed(range(count.bit_length() - 1))]
    doubling = count & (count - 1) == 0
    if doubling:
        panel = widen(panel, bits[:2], count)
    packed, panel = lax.optimization_barrier((packed, panel))
    got = lax.all_to_all(packed, "wide", split_axis=0, concat_axis=0, tiled=True)
    if doubling:
        for bit in bits[2:]:
            panel = widen(panel, [bit], count)
    else:
        panel = lax.all_gather(panel, "wide", axis=0, tiled=True)
    panel = panel.reshape(basis, -1)
    return contract(got, weights(panel, pattern, parts), parts, groups, height, per)


def on_device(count, narrow, integrals, fitted, occupied, pattern):
    aux, per, basis = integrals.shape
    groups = next(g for g in (FULL, FULL // 2, 1) if aux // count * per % (16 * g) == 0)
    choices = [(cap, parts_of(cap, groups)) for cap in range(1, NBLK + 1)]
    choices = [(cap, parts) for cap, parts in choices if parts is not None]
    choice = choose(pattern, [cap for cap, _ in choices[:-1]])
    branches = [functools.partial(share, parts, groups, count) for _, parts in choices]
    total = lax.switch(choice, branches, integrals, fitted, occupied, pattern)
    strips = lax.all_to_all(total.reshape(count, per, basis), "wide", split_axis=0, concat_axis=0, tiled=True)
    strip = jnp.sum(strips.reshape(count, per, basis), axis=0)
    return lax.psum(strip, "narrow") if narrow > 1 else strip


def solution(mesh):
    in_specs = (P("narrow", "wide", None), P("narrow", "wide", None), P("wide", None), P())
    out_specs = P("wide", None)
    body = functools.partial(on_device, mesh.shape["wide"], mesh.shape["narrow"])
    return jax.shard_map(body, mesh=mesh, in_specs=in_specs, out_specs=out_specs, check_vma=False)
```

```python
import functools

import jax
import jax.numpy as jnp
import numpy as np
from jax import lax
from jax.experimental import pallas as pl
from jax.experimental.pallas import tpu as pltpu
from jax.sharding import PartitionSpec as P

NBLK = 8
FULL = NBLK // 2
DEPTH = 2048
VMEM = 62 * 2**20
SORT_VMEM = 24 * 2**20
NT = (((1,), (1,)), ((), ()))
PLANES = NBLK // 2
PLANS = ((5, 0), (4, 2), (6, 0), (5, 2), (7, 0), (8, 0))


def parts_of(cap, groups):
    parts = []
    for piece in (FULL, FULL, FULL // 2, FULL // 4):
        if cap >= piece and FULL // piece <= groups:
            parts.append(piece)
            cap -= piece
    return parts if cap == 0 else None


def with_extra(parts, extra):
    return list(parts) + [extra] * (extra > 0)


def lane_layout(parts, extra, basis):
    width = basis // NBLK
    lane = np.arange(basis)
    slot, base, offset = [], [], 0
    for piece in with_extra(parts, extra):
        inner = lane % (basis * piece // FULL)
        slot.append(offset + inner % (piece * width) // width)
        base.append(inner // (piece * width) * basis + inner % width)
        offset += piece
    slot = np.concatenate(slot)
    return np.stack([slot, np.concatenate(base), slot >= sum(parts)]).astype(np.int32)


def surplus(pattern_ref, block, direct):
    alive = jnp.int32(0)
    for other in range(NBLK):
        alive = alive + (pattern_ref[block, other] != 0).astype(jnp.int32)
    return jnp.maximum(alive - direct, 0)


def columns_of(pattern_ref, block, slot, base, width):
    columns = jnp.full(slot.shape, -1, jnp.int32)
    rank = jnp.int32(0)
    for other in range(NBLK):
        alive = pattern_ref[block, other] != 0
        columns = jnp.where(slot == jnp.where(alive, rank, -1), base + other * width, columns)
        rank = rank + alive.astype(jnp.int32)
    return columns


def halves(wide):
    high = wide.astype(jnp.bfloat16)
    return high, (wide - high.astype(jnp.float32)).astype(jnp.bfloat16)


def pack_kernel(parts, extra, groups, me_ref, pattern_ref, layout_ref, ints_hbm, fitted_hbm, *refs):
    out_hbm, over_hbm, (both, out, table, in_sems, out_sems) = refs[0], refs[1:-5], refs[-5:]
    count, rows, lanes = both.shape
    basis = lanes // 2
    chunks = count // PLANES
    step = rows // groups
    direct_rows = out_hbm.shape[1]
    extra_rows = out.shape[1] - direct_rows
    place = lax.rem(me_ref[0], chunks)

    def arrivals(turn):
        here = pl.ds(turn * chunks, chunks)
        return (
            pltpu.make_async_copy(ints_hbm.at[here], both.at[here, :, pl.ds(0, basis)], in_sems.at[turn, 0]),
            pltpu.make_async_copy(fitted_hbm.at[here], both.at[here, :, pl.ds(basis, basis)], in_sems.at[turn, 1]),
        )

    def departures(turn):
        here = pl.ds(turn * chunks, chunks)
        copies = [pltpu.make_async_copy(out.at[here, pl.ds(0, direct_rows)], out_hbm.at[here], out_sems.at[turn, 0])]
        for apart, ref in enumerate(over_hbm):
            source = out.at[turn * chunks + lax.bitwise_xor(place, apart), pl.ds(direct_rows, extra_rows)]
            copies.append(pltpu.make_async_copy(source, ref.at[turn], out_sems.at[turn, 1 + apart]))
        return copies

    for turn in range(PLANES):
        for copy in arrivals(turn):
            copy.start()

    layout = layout_ref[...]
    block = lax.div(me_ref[0] * NBLK, count)
    columns = columns_of(pattern_ref, block, layout[0:1], layout[1:2], basis // NBLK)
    height = lax.broadcasted_iota(jnp.int32, table.shape, 0)
    table[...] = jnp.where(height == columns, 1.0, 0.0).astype(jnp.bfloat16)

    lane = lax.broadcasted_iota(jnp.int32, (chunks * step, basis), 1)

    def work(turn, _):
        for copy in arrivals(turn):
            copy.wait()
        here = pl.ds(turn * chunks, chunks)
        packed = []
        for group in range(groups):
            mine = both[here, pl.ds(group * step, step), :].reshape(chunks * step, lanes)
            packed.append(jnp.dot(mine, table[...], preferred_element_type=jnp.float32))
        start = 0
        for index, piece in enumerate(with_extra(parts, extra)):
            shared = FULL // piece
            held = slice(index * basis, (index + 1) * basis)
            for inner in range(groups // shared):
                total = packed[inner][:, held]
                for other in range(1, shared):
                    theirs = packed[other * (groups // shared) + inner][:, held]
                    total = jnp.where(lane >= other * (basis // shared), theirs, total)
                out[here, pl.ds(start, step), :] = total.astype(jnp.bfloat16).reshape(chunks, step, basis)
                start += step
        for copy in departures(turn):
            copy.start()
        return 0

    lax.fori_loop(0, PLANES, work, 0)
    for turn in range(PLANES):
        for copy in departures(turn):
            copy.wait()


def pack(ints, fitted, me, pattern, parts, extra, groups):
    count, rows, basis = ints.shape
    direct_rows = sum(rows * piece // FULL for piece in parts)
    extra_rows = rows * extra // FULL
    plane = count // PLANES
    layout = lane_layout(parts, extra, basis)
    flops = 2 * count * rows * 2 * basis * layout.shape[1]
    moved = 2 * ints.nbytes + 2 * count * (direct_rows + extra_rows) * basis
    shapes = [jax.ShapeDtypeStruct((count, direct_rows, basis), jnp.bfloat16)]
    if extra:
        shapes += [jax.ShapeDtypeStruct((PLANES, extra_rows, basis), jnp.bfloat16)] * plane
    return pl.pallas_call(
        functools.partial(pack_kernel, parts, extra, groups),
        out_shape=shapes,
        in_specs=[
            pl.BlockSpec(memory_space=pltpu.SMEM),
            pl.BlockSpec(memory_space=pltpu.SMEM),
            pl.BlockSpec(memory_space=pltpu.VMEM),
            pl.BlockSpec(memory_space=pl.ANY),
            pl.BlockSpec(memory_space=pl.ANY),
        ],
        out_specs=[pl.BlockSpec(memory_space=pl.ANY)] * len(shapes),
        scratch_shapes=[
            pltpu.VMEM((count, rows, 2 * basis), jnp.bfloat16),
            pltpu.VMEM((count, direct_rows + extra_rows, basis), jnp.bfloat16),
            pltpu.VMEM((2 * basis, layout.shape[1]), jnp.bfloat16),
            pltpu.SemaphoreType.DMA((PLANES, 2)),
            pltpu.SemaphoreType.DMA((PLANES, len(shapes))),
        ],
        compiler_params=pltpu.CompilerParams(vmem_limit_bytes=VMEM),
        cost_estimate=pl.CostEstimate(flops=flops, bytes_accessed=moved, transcendentals=0),
        name="pack",
    )(me, pattern, jnp.asarray(layout), ints, fitted)


def sort_kernel(direct, me_ref, pattern_ref, slot_ref, over_ref, out_ref):
    planes, sources, _, basis = out_ref.shape
    plane = 2 * sources
    place, level = lax.rem(me_ref[0], plane), lax.div(me_ref[0], plane)
    first = surplus(pattern_ref, 2 * level, direct)
    row = lax.broadcasted_iota(jnp.int32, (basis, basis), 0)
    column = lax.broadcasted_iota(jnp.int32, (basis, basis), 1)
    slot = slot_ref[0:1]
    stay = jnp.where((row == column) & (slot < first), 1.0, 0.0)
    move = jnp.where((row == column - first * (basis // NBLK)) & (slot >= first), 1.0, 0.0)
    table = jnp.concatenate([stay, move], axis=0).astype(jnp.bfloat16)

    def work(away, _):
        there = lax.bitwise_xor(level, away)
        for source in range(sources):
            pair = [over_ref[lax.bitwise_xor(place, second * sources + source), there] for second in range(2)]
            sorted_rows = jnp.dot(jnp.concatenate(pair, axis=1), table, preferred_element_type=jnp.float32)
            out_ref[away, source] = sorted_rows.astype(jnp.bfloat16)
        return 0

    lax.fori_loop(0, planes, work, 0)


def sort(over, me, pattern, direct, extra):
    plane, _, rows, basis = over.shape
    slots = lane_layout((extra,), 0, basis)
    flops = 4 * PLANES * plane // 2 * rows * basis * basis
    return pl.pallas_call(
        functools.partial(sort_kernel, direct),
        out_shape=jax.ShapeDtypeStruct((PLANES, plane // 2, rows, basis), jnp.bfloat16),
        in_specs=[pl.BlockSpec(memory_space=pltpu.SMEM)] * 2 + [pl.BlockSpec(memory_space=pltpu.VMEM)] * 2,
        out_specs=pl.BlockSpec(memory_space=pltpu.VMEM),
        compiler_params=pltpu.CompilerParams(vmem_limit_bytes=SORT_VMEM),
        cost_estimate=pl.CostEstimate(flops=flops, bytes_accessed=2 * over.nbytes, transcendentals=0),
        name="sort",
    )(me, pattern, jnp.asarray(slots), over)


def weights_kernel(direct, pattern_ref, layout_ref, panel_ref, out_ref):
    basis = panel_ref.shape[0]
    lanes = layout_ref.shape[0]
    panel = panel_ref[...]
    gram = lax.dot_general(panel, panel, NT, preferred_element_type=jnp.float32)
    high, low = halves(gram)
    column = lax.broadcasted_iota(jnp.int32, (lanes, 2 * basis), 1)

    def fill(block, _):
        before = lax.rem(block, 2) * surplus(pattern_ref, block - lax.rem(block, 2), direct)
        slot = layout_ref[:, 0:1] - layout_ref[:, 2:3] * before
        slot = jnp.where((layout_ref[:, 2:3] == 0) | (slot >= direct), slot, -2)
        held = columns_of(pattern_ref, block, slot, layout_ref[:, 1:2], basis // NBLK)
        table = jnp.where(column == held, 1.0, 0.0).astype(jnp.bfloat16)
        ints = table[:, :basis]
        out_ref[block, :lanes, :basis] = jnp.dot(ints, high, preferred_element_type=jnp.float32).astype(jnp.bfloat16)
        out_ref[block, :lanes, basis:] = table[:, basis:]
        out_ref[block, lanes:, :basis] = jnp.dot(ints, low, preferred_element_type=jnp.float32).astype(jnp.bfloat16)
        out_ref[block, lanes:, basis:] = jnp.zeros((lanes, basis), jnp.bfloat16)
        return 0

    lax.fori_loop(0, NBLK, fill, 0)


def weights(panel, pattern, parts, extra):
    basis = panel.shape[0]
    layout = lane_layout(parts, extra, basis).T
    lanes = layout.shape[0]
    return pl.pallas_call(
        functools.partial(weights_kernel, sum(parts)),
        out_shape=jax.ShapeDtypeStruct((NBLK, 2 * lanes, 2 * basis), jnp.bfloat16),
        in_specs=[
            pl.BlockSpec(memory_space=pltpu.SMEM),
            pl.BlockSpec(memory_space=pltpu.VMEM),
            pl.BlockSpec(memory_space=pltpu.VMEM),
        ],
        out_specs=pl.BlockSpec(memory_space=pltpu.VMEM),
        compiler_params=pltpu.CompilerParams(vmem_limit_bytes=VMEM),
        cost_estimate=pl.CostEstimate(flops=2 * NBLK * 2 * lanes * basis * basis, bytes_accessed=2 * panel.nbytes, transcendentals=0),
        name="weights",
    )(pattern, jnp.asarray(layout), panel)


def contract_kernel(parts, extra, groups, per, me_ref, tables_hbm, got_hbm, *refs):
    more_hbm = refs[: PLANES if extra else 0]
    out_ref, tables, got, more, left, right, sems, more_sems = refs[len(more_hbm) :]
    count, _, basis = got.shape
    sources = count // NBLK
    height = right.shape[1] // basis * 8
    step = height // groups
    wide = count * 8

    def arrivals(block):
        here = pl.ds(block * sources, sources)
        return (
            pltpu.make_async_copy(tables_hbm.at[block], tables.at[block], sems.at[block, 0]),
            pltpu.make_async_copy(got_hbm.at[here], got.at[here], sems.at[block, 1]),
        )

    def more_arrival(away):
        level = lax.bitwise_xor(lax.div(me_ref[0] * PLANES, count), away)
        return pltpu.make_async_copy(more_hbm[away], more.at[level], more_sems.at[away])

    for block in range(NBLK):
        for copy in arrivals(block):
            copy.start()
        if extra and block == 0:
            for away in range(PLANES):
                more_arrival(away).start()
    for away in range(len(more_hbm)):
        more_arrival(away).wait()

    def unpack(block, _):
        for copy in arrivals(block):
            copy.wait()
        here = pl.ds(block * sources, sources)
        pieces, start = [], 0
        for index, piece in enumerate(with_extra(parts, extra)):
            shared = FULL // piece
            kept = groups // shared * step
            if index < len(parts):
                part = got[here, pl.ds(start, kept), :]
            else:
                part = more[lax.div(block, 2)]
            start += kept
            if shared > 1:
                lane = lax.broadcasted_iota(jnp.int32, part.shape, 2)
                window = basis // shared
                part = jnp.concatenate(
                    [
                        jnp.where((lane >= own * window) & (lane < (own + 1) * window), part, jnp.zeros_like(part))
                        for own in range(shared)
                    ],
                    axis=1,
                )
            pieces.append(part.reshape(sources * height, basis))
        both = jnp.concatenate(pieces + pieces, axis=1)
        turned = jnp.dot(both, tables[block], preferred_element_type=jnp.float32).reshape(sources, height, 2 * basis)
        rows = pl.ds(pl.multiple_of(block * (sources * 8), sources * 8), sources * 8)
        low_rows = pl.ds(pl.multiple_of(block * (sources * 8) + wide, sources * 8), sources * 8)
        for eight in range(height // 8):
            lanes = slice(eight * basis, (eight + 1) * basis)
            mine = turned[:, eight * 8 : eight * 8 + 8, :].reshape(sources * 8, 2 * basis)
            high = mine[:, :basis].astype(jnp.bfloat16)
            left[rows, lanes] = high
            left[low_rows, lanes] = (mine[:, :basis] - high.astype(jnp.float32)).astype(jnp.bfloat16)
            right[rows, lanes] = mine[:, basis:].astype(jnp.bfloat16)
        return 0

    lax.fori_loop(0, NBLK, unpack, 0)
    turns = right.shape[1] // DEPTH if right.shape[1] % DEPTH == 0 else 1
    depth = right.shape[1] // turns

    def multiply(turn, sums):
        lanes = pl.ds(pl.multiple_of(turn * depth, depth), depth)
        return sums + lax.dot_general(left[:, lanes], right[:, lanes], NT, preferred_element_type=jnp.float32)

    total = lax.fori_loop(0, turns, multiply, jnp.zeros((2 * wide, wide), jnp.float32))
    total = total[:wide] + total[wide:]
    row = lax.broadcasted_iota(jnp.int32, (wide, wide), 0) % 8 // per
    column = lax.broadcasted_iota(jnp.int32, (wide, wide), 1) % 8 // per
    total = jnp.where(row == column, total, 0.0)
    spot = lax.broadcasted_iota(jnp.int32, (basis, wide), 1)
    spot = spot // 8 * per + spot % per
    fold = jnp.where(spot == lax.broadcasted_iota(jnp.int32, (basis, wide), 0), 1.0, 0.0).astype(jnp.bfloat16)
    high, low = halves(total)
    total = jnp.dot(fold, high, preferred_element_type=jnp.float32) + jnp.dot(
        fold, low, preferred_element_type=jnp.float32
    )
    high, low = halves(total)
    total = lax.dot_general(high, fold, NT, preferred_element_type=jnp.float32) + lax.dot_general(
        low, fold, NT, preferred_element_type=jnp.float32
    )
    out_ref[...] = total + total.T


def contract(me, got, more, tables, parts, extra, groups, height, per):
    count, _, basis = got.shape
    deep = height // 8 * basis
    return pl.pallas_call(
        functools.partial(contract_kernel, parts, extra, groups, per),
        out_shape=jax.ShapeDtypeStruct((basis, basis), jnp.float32),
        in_specs=[pl.BlockSpec(memory_space=pltpu.SMEM)] + [pl.BlockSpec(memory_space=pl.ANY)] * (2 + len(more)),
        out_specs=pl.BlockSpec(memory_space=pltpu.VMEM),
        scratch_shapes=[
            pltpu.VMEM(tables.shape, jnp.bfloat16),
            pltpu.VMEM(got.shape, jnp.bfloat16),
            pltpu.VMEM((PLANES,) + (more[0].shape if extra else (8, basis)), jnp.bfloat16),
            pltpu.VMEM((count * 16, deep), jnp.bfloat16),
            pltpu.VMEM((count * 8, deep), jnp.bfloat16),
            pltpu.SemaphoreType.DMA((NBLK, 2)),
            pltpu.SemaphoreType.DMA((PLANES,)),
        ],
        compiler_params=pltpu.CompilerParams(vmem_limit_bytes=VMEM),
        name="contract",
    )(me, tables, got, *more)


def swap(rows, mask, count):
    return lax.ppermute(rows, "wide", [(i, i ^ mask) for i in range(count)]) if mask else rows


def widen(rows, bits, count):
    me, size = lax.axis_index("wide"), 2 ** len(bits)
    masks = [sum(bit for place, bit in enumerate(reversed(bits)) if turn >> place & 1) for turn in range(size)]
    got = [swap(rows, mask, count) for mask in masks]
    for place, bit in enumerate(reversed(bits)):
        low = me // bit % 2 == 0
        got = [jnp.where(low, got[turn], got[turn ^ 1 << place]) for turn in range(size)]
    return jnp.stack(got, axis=1).reshape((-1,) + rows.shape[1:])


def choose(pattern, plans):
    def kernel(pattern_ref, out_ref):
        alive = [surplus(pattern_ref, block, 0) for block in range(NBLK)]
        choice = jnp.int32(len(plans) - 1)
        for index, (direct, extra) in reversed(list(enumerate(plans[:-1]))):
            needed = jnp.int32(0)
            for level in range(PLANES):
                pair = jnp.maximum(alive[2 * level] - direct, 0) + jnp.maximum(alive[2 * level + 1] - direct, 0)
                needed = jnp.maximum(needed, pair)
            choice = jnp.where(needed <= extra, index, choice)
        out_ref[0] = choice

    return pl.pallas_call(
        kernel,
        out_shape=jax.ShapeDtypeStruct((1,), jnp.int32),
        in_specs=[pl.BlockSpec(memory_space=pltpu.SMEM)],
        out_specs=pl.BlockSpec(memory_space=pltpu.SMEM),
        name="choose",
    )(pattern)[0]


def share(parts, extra, groups, count, integrals, fitted, occupied, pattern):
    aux, per, basis = integrals.shape
    height = aux // count * per
    plane = count // PLANES
    me = lax.axis_index("wide").astype(jnp.int32).reshape(1)
    packed, *over = pack(
        integrals.reshape(count, height, basis), fitted.reshape(count, height, basis), me, pattern, parts, extra, groups
    )
    panel = occupied[None]
    bits = [1 << place for place in reversed(range(count.bit_length() - 1))]
    doubling = count & (count - 1) == 0
    if doubling:
        panel = widen(panel, bits[:2], count)
    packed, panel, over = lax.optimization_barrier((packed, panel, over))
    got = lax.all_to_all(packed, "wide", split_axis=0, concat_axis=0, tiled=True)
    more = []
    if extra:
        over = [swap(rows, apart, count) for apart, rows in enumerate(over)]
        sorted_rows = sort(jnp.stack(over), me, pattern, sum(parts), extra)
        more = [swap(sorted_rows[away], away * plane, count) for away in range(PLANES)]
    if doubling:
        panel = widen(panel, bits[2:], count)
    else:
        panel = lax.all_gather(panel, "wide", axis=0, tiled=True)
    tables = weights(panel.reshape(basis, -1), pattern, parts, extra)
    return contract(me, got, more, tables, parts, extra, groups, height, per)


def on_device(count, narrow, integrals, fitted, occupied, pattern):
    aux, per, basis = integrals.shape
    groups = next(g for g in (FULL, FULL // 2, 1) if aux // count * per % (16 * g) == 0)
    paired = groups == FULL and count & (count - 1) == 0
    plans = PLANS if paired else [(direct, 0) for direct in range(1, NBLK + 1) if parts_of(direct, groups)]
    branches = [functools.partial(share, parts_of(direct, groups), extra, groups, count) for direct, extra in plans]
    total = lax.switch(choose(pattern, plans), branches, integrals, fitted, occupied, pattern)
    strips = lax.all_to_all(total.reshape(count, per, basis), "wide", split_axis=0, concat_axis=0, tiled=True)
    strip = jnp.sum(strips.reshape(count, per, basis), axis=0)
    return lax.psum(strip, "narrow") if narrow > 1 else strip


def solution(mesh):
    in_specs = (P("narrow", "wide", None), P("narrow", "wide", None), P("wide", None), P())
    out_specs = P("wide", None)
    body = functools.partial(on_device, mesh.shape["wide"], mesh.shape["narrow"])
    return jax.shard_map(body, mesh=mesh, in_specs=in_specs, out_specs=out_specs, check_vma=False)
```

```python
import functools

import jax
import jax.numpy as jnp
import numpy as np
from jax import lax
from jax.experimental import pallas as pl
from jax.experimental.pallas import tpu as pltpu
from jax.sharding import PartitionSpec as P

NBLK = 8
FULL = NBLK // 2
DEPTH = 2048
VMEM = 62 * 2**20
SORT_VMEM = 24 * 2**20
NT = (((1,), (1,)), ((), ()))
PLANES = NBLK // 2
PLANS = ((4, 1), (5, 0), (4, 2), (6, 0), (5, 2), (7, 0), (8, 0))


def parts_of(cap, groups):
    parts = []
    for piece in (FULL, FULL, FULL // 2, FULL // 4):
        if cap >= piece and FULL // piece <= groups:
            parts.append(piece)
            cap -= piece
    return parts if cap == 0 else None


def with_extra(parts, extra):
    return list(parts) + [extra] * (extra > 0)


def lane_layout(parts, extra, basis):
    width = basis // NBLK
    lane = np.arange(basis)
    slot, base, offset = [], [], 0
    for piece in with_extra(parts, extra):
        inner = lane % (basis * piece // FULL)
        slot.append(offset + inner % (piece * width) // width)
        base.append(inner // (piece * width) * basis + inner % width)
        offset += piece
    slot = np.concatenate(slot)
    return np.stack([slot, np.concatenate(base), slot >= sum(parts)]).astype(np.int32)


def surplus(pattern_ref, block, direct):
    alive = jnp.int32(0)
    for other in range(NBLK):
        alive = alive + (pattern_ref[block, other] != 0).astype(jnp.int32)
    return jnp.maximum(alive - direct, 0)


def columns_of(pattern_ref, block, slot, base, width):
    columns = jnp.full(slot.shape, -1, jnp.int32)
    rank = jnp.int32(0)
    for other in range(NBLK):
        alive = pattern_ref[block, other] != 0
        columns = jnp.where(slot == jnp.where(alive, rank, -1), base + other * width, columns)
        rank = rank + alive.astype(jnp.int32)
    return columns


def halves(wide):
    high = wide.astype(jnp.bfloat16)
    return high, (wide - high.astype(jnp.float32)).astype(jnp.bfloat16)


def pack_kernel(parts, extra, groups, me_ref, pattern_ref, layout_ref, ints_hbm, fitted_hbm, *refs):
    out_hbm, over_hbm, (both, out, table, in_sems, out_sems) = refs[0], refs[1:-5], refs[-5:]
    count, rows, lanes = both.shape
    basis = lanes // 2
    chunks = count // PLANES
    step = rows // groups
    direct_rows = out_hbm.shape[1]
    extra_rows = out.shape[1] - direct_rows
    place = lax.rem(me_ref[0], chunks)

    def arrivals(turn):
        here = pl.ds(turn * chunks, chunks)
        return (
            pltpu.make_async_copy(ints_hbm.at[here], both.at[here, :, pl.ds(0, basis)], in_sems.at[turn, 0]),
            pltpu.make_async_copy(fitted_hbm.at[here], both.at[here, :, pl.ds(basis, basis)], in_sems.at[turn, 1]),
        )

    def departures(turn):
        here = pl.ds(turn * chunks, chunks)
        copies = [pltpu.make_async_copy(out.at[here, pl.ds(0, direct_rows)], out_hbm.at[here], out_sems.at[turn, 0])]
        for apart, ref in enumerate(over_hbm):
            source = out.at[turn * chunks + lax.bitwise_xor(place, apart), pl.ds(direct_rows, extra_rows)]
            copies.append(pltpu.make_async_copy(source, ref.at[turn], out_sems.at[turn, 1 + apart]))
        return copies

    for turn in range(PLANES):
        for copy in arrivals(turn):
            copy.start()

    layout = layout_ref[...]
    block = lax.div(me_ref[0] * NBLK, count)
    columns = columns_of(pattern_ref, block, layout[0:1], layout[1:2], basis // NBLK)
    height = lax.broadcasted_iota(jnp.int32, table.shape, 0)
    table[...] = jnp.where(height == columns, 1.0, 0.0).astype(jnp.bfloat16)

    lane = lax.broadcasted_iota(jnp.int32, (chunks * step, basis), 1)

    def work(turn, _):
        for copy in arrivals(turn):
            copy.wait()
        here = pl.ds(turn * chunks, chunks)
        packed = []
        for group in range(groups):
            mine = both[here, pl.ds(group * step, step), :].reshape(chunks * step, lanes)
            packed.append(jnp.dot(mine, table[...], preferred_element_type=jnp.float32))
        start = 0
        for index, piece in enumerate(with_extra(parts, extra)):
            shared = FULL // piece
            held = slice(index * basis, (index + 1) * basis)
            for inner in range(groups // shared):
                total = packed[inner][:, held]
                for other in range(1, shared):
                    theirs = packed[other * (groups // shared) + inner][:, held]
                    total = jnp.where(lane >= other * (basis // shared), theirs, total)
                out[here, pl.ds(start, step), :] = total.astype(jnp.bfloat16).reshape(chunks, step, basis)
                start += step
        for copy in departures(turn):
            copy.start()
        return 0

    lax.fori_loop(0, PLANES, work, 0)
    for turn in range(PLANES):
        for copy in departures(turn):
            copy.wait()


def pack(ints, fitted, me, pattern, parts, extra, groups):
    count, rows, basis = ints.shape
    direct_rows = sum(rows * piece // FULL for piece in parts)
    extra_rows = rows * extra // FULL
    plane = count // PLANES
    layout = lane_layout(parts, extra, basis)
    flops = 2 * count * rows * 2 * basis * layout.shape[1]
    moved = 2 * ints.nbytes + 2 * count * (direct_rows + extra_rows) * basis
    shapes = [jax.ShapeDtypeStruct((count, direct_rows, basis), jnp.bfloat16)]
    if extra:
        shapes += [jax.ShapeDtypeStruct((PLANES, extra_rows, basis), jnp.bfloat16)] * plane
    return pl.pallas_call(
        functools.partial(pack_kernel, parts, extra, groups),
        out_shape=shapes,
        in_specs=[
            pl.BlockSpec(memory_space=pltpu.SMEM),
            pl.BlockSpec(memory_space=pltpu.SMEM),
            pl.BlockSpec(memory_space=pltpu.VMEM),
            pl.BlockSpec(memory_space=pl.ANY),
            pl.BlockSpec(memory_space=pl.ANY),
        ],
        out_specs=[pl.BlockSpec(memory_space=pl.ANY)] * len(shapes),
        scratch_shapes=[
            pltpu.VMEM((count, rows, 2 * basis), jnp.bfloat16),
            pltpu.VMEM((count, direct_rows + extra_rows, basis), jnp.bfloat16),
            pltpu.VMEM((2 * basis, layout.shape[1]), jnp.bfloat16),
            pltpu.SemaphoreType.DMA((PLANES, 2)),
            pltpu.SemaphoreType.DMA((PLANES, len(shapes))),
        ],
        compiler_params=pltpu.CompilerParams(vmem_limit_bytes=VMEM),
        cost_estimate=pl.CostEstimate(flops=flops, bytes_accessed=moved, transcendentals=0),
        name="pack",
    )(me, pattern, jnp.asarray(layout), ints, fitted)


def sort_kernel(direct, me_ref, pattern_ref, slot_ref, over_ref, out_ref):
    planes, sources, _, basis = out_ref.shape
    plane = 2 * sources
    place, level = lax.rem(me_ref[0], plane), lax.div(me_ref[0], plane)
    first = surplus(pattern_ref, 2 * level, direct)
    row = lax.broadcasted_iota(jnp.int32, (basis, basis), 0)
    column = lax.broadcasted_iota(jnp.int32, (basis, basis), 1)
    slot = slot_ref[0:1]
    stay = jnp.where((row == column) & (slot < first), 1.0, 0.0)
    move = jnp.where((row == column - first * (basis // NBLK)) & (slot >= first), 1.0, 0.0)
    table = jnp.concatenate([stay, move], axis=0).astype(jnp.bfloat16)

    def work(away, _):
        there = lax.bitwise_xor(level, away)
        for source in range(sources):
            pair = [over_ref[lax.bitwise_xor(place, second * sources + source), there] for second in range(2)]
            sorted_rows = jnp.dot(jnp.concatenate(pair, axis=1), table, preferred_element_type=jnp.float32)
            out_ref[away, source] = sorted_rows.astype(jnp.bfloat16)
        return 0

    lax.fori_loop(0, planes, work, 0)


def sort(over, me, pattern, direct, extra):
    plane, _, rows, basis = over.shape
    slots = lane_layout((extra,), 0, basis)
    flops = 4 * PLANES * plane // 2 * rows * basis * basis
    return pl.pallas_call(
        functools.partial(sort_kernel, direct),
        out_shape=jax.ShapeDtypeStruct((PLANES, plane // 2, rows, basis), jnp.bfloat16),
        in_specs=[pl.BlockSpec(memory_space=pltpu.SMEM)] * 2 + [pl.BlockSpec(memory_space=pltpu.VMEM)] * 2,
        out_specs=pl.BlockSpec(memory_space=pltpu.VMEM),
        compiler_params=pltpu.CompilerParams(vmem_limit_bytes=SORT_VMEM),
        cost_estimate=pl.CostEstimate(flops=flops, bytes_accessed=2 * over.nbytes, transcendentals=0),
        name="sort",
    )(me, pattern, jnp.asarray(slots), over)


def weights_kernel(direct, pattern_ref, layout_ref, panel_ref, out_ref):
    basis = panel_ref.shape[0]
    lanes = layout_ref.shape[0]
    panel = panel_ref[...]
    gram = lax.dot_general(panel, panel, NT, preferred_element_type=jnp.float32)
    high, low = halves(gram)
    column = lax.broadcasted_iota(jnp.int32, (lanes, 2 * basis), 1)

    def fill(block, _):
        before = lax.rem(block, 2) * surplus(pattern_ref, block - lax.rem(block, 2), direct)
        slot = layout_ref[:, 0:1] - layout_ref[:, 2:3] * before
        slot = jnp.where((layout_ref[:, 2:3] == 0) | (slot >= direct), slot, -2)
        held = columns_of(pattern_ref, block, slot, layout_ref[:, 1:2], basis // NBLK)
        table = jnp.where(column == held, 1.0, 0.0).astype(jnp.bfloat16)
        ints = table[:, :basis]
        out_ref[block, :lanes, :basis] = jnp.dot(ints, high, preferred_element_type=jnp.float32).astype(jnp.bfloat16)
        out_ref[block, :lanes, basis:] = table[:, basis:]
        out_ref[block, lanes:, :basis] = jnp.dot(ints, low, preferred_element_type=jnp.float32).astype(jnp.bfloat16)
        out_ref[block, lanes:, basis:] = jnp.zeros((lanes, basis), jnp.bfloat16)
        return 0

    lax.fori_loop(0, NBLK, fill, 0)


def weights(panel, pattern, parts, extra):
    basis = panel.shape[0]
    layout = lane_layout(parts, extra, basis).T
    lanes = layout.shape[0]
    return pl.pallas_call(
        functools.partial(weights_kernel, sum(parts)),
        out_shape=jax.ShapeDtypeStruct((NBLK, 2 * lanes, 2 * basis), jnp.bfloat16),
        in_specs=[
            pl.BlockSpec(memory_space=pltpu.SMEM),
            pl.BlockSpec(memory_space=pltpu.VMEM),
            pl.BlockSpec(memory_space=pltpu.VMEM),
        ],
        out_specs=pl.BlockSpec(memory_space=pltpu.VMEM),
        compiler_params=pltpu.CompilerParams(vmem_limit_bytes=VMEM),
        cost_estimate=pl.CostEstimate(flops=2 * NBLK * 2 * lanes * basis * basis, bytes_accessed=2 * panel.nbytes, transcendentals=0),
        name="weights",
    )(pattern, jnp.asarray(layout), panel)


def contract_kernel(parts, extra, groups, per, me_ref, tables_hbm, got_hbm, *refs):
    more_hbm = refs[: PLANES if extra else 0]
    out_ref, tables, got, more, left, right, sems, more_sems = refs[len(more_hbm) :]
    count, _, basis = got.shape
    sources = count // NBLK
    height = right.shape[1] // basis * 8
    step = height // groups
    wide = count * 8

    def arrivals(block):
        here = pl.ds(block * sources, sources)
        return (
            pltpu.make_async_copy(tables_hbm.at[block], tables.at[block], sems.at[block, 0]),
            pltpu.make_async_copy(got_hbm.at[here], got.at[here], sems.at[block, 1]),
        )

    def more_arrival(away):
        level = lax.bitwise_xor(lax.div(me_ref[0] * PLANES, count), away)
        return pltpu.make_async_copy(more_hbm[away], more.at[level], more_sems.at[away])

    for block in range(NBLK):
        for copy in arrivals(block):
            copy.start()
        if extra and block == 0:
            for away in range(PLANES):
                more_arrival(away).start()
    for away in range(len(more_hbm)):
        more_arrival(away).wait()

    def unpack(block, _):
        for copy in arrivals(block):
            copy.wait()
        here = pl.ds(block * sources, sources)
        pieces, start = [], 0
        for index, piece in enumerate(with_extra(parts, extra)):
            shared = FULL // piece
            kept = groups // shared * step
            if index < len(parts):
                part = got[here, pl.ds(start, kept), :]
            else:
                part = more[lax.div(block, 2)]
            start += kept
            if shared > 1:
                lane = lax.broadcasted_iota(jnp.int32, part.shape, 2)
                window = basis // shared
                part = jnp.concatenate(
                    [
                        jnp.where((lane >= own * window) & (lane < (own + 1) * window), part, jnp.zeros_like(part))
                        for own in range(shared)
                    ],
                    axis=1,
                )
            pieces.append(part.reshape(sources * height, basis))
        both = jnp.concatenate(pieces + pieces, axis=1)
        turned = jnp.dot(both, tables[block], preferred_element_type=jnp.float32).reshape(sources, height, 2 * basis)
        rows = pl.ds(pl.multiple_of(block * (sources * 8), sources * 8), sources * 8)
        low_rows = pl.ds(pl.multiple_of(block * (sources * 8) + wide, sources * 8), sources * 8)
        for eight in range(height // 8):
            lanes = slice(eight * basis, (eight + 1) * basis)
            mine = turned[:, eight * 8 : eight * 8 + 8, :].reshape(sources * 8, 2 * basis)
            high = mine[:, :basis].astype(jnp.bfloat16)
            left[rows, lanes] = high
            left[low_rows, lanes] = (mine[:, :basis] - high.astype(jnp.float32)).astype(jnp.bfloat16)
            right[rows, lanes] = mine[:, basis:].astype(jnp.bfloat16)
        return 0

    lax.fori_loop(0, NBLK, unpack, 0)
    turns = right.shape[1] // DEPTH if right.shape[1] % DEPTH == 0 else 1
    depth = right.shape[1] // turns

    def multiply(turn, sums):
        lanes = pl.ds(pl.multiple_of(turn * depth, depth), depth)
        return sums + lax.dot_general(left[:, lanes], right[:, lanes], NT, preferred_element_type=jnp.float32)

    total = lax.fori_loop(0, turns, multiply, jnp.zeros((2 * wide, wide), jnp.float32))
    total = total[:wide] + total[wide:]
    row = lax.broadcasted_iota(jnp.int32, (wide, wide), 0) % 8 // per
    column = lax.broadcasted_iota(jnp.int32, (wide, wide), 1) % 8 // per
    total = jnp.where(row == column, total, 0.0)
    spot = lax.broadcasted_iota(jnp.int32, (basis, wide), 1)
    spot = spot // 8 * per + spot % per
    fold = jnp.where(spot == lax.broadcasted_iota(jnp.int32, (basis, wide), 0), 1.0, 0.0).astype(jnp.bfloat16)
    high, low = halves(total)
    total = jnp.dot(fold, high, preferred_element_type=jnp.float32) + jnp.dot(
        fold, low, preferred_element_type=jnp.float32
    )
    high, low = halves(total)
    total = lax.dot_general(high, fold, NT, preferred_element_type=jnp.float32) + lax.dot_general(
        low, fold, NT, preferred_element_type=jnp.float32
    )
    out_ref[...] = total + total.T


def contract(me, got, more, tables, parts, extra, groups, height, per):
    count, _, basis = got.shape
    deep = height // 8 * basis
    return pl.pallas_call(
        functools.partial(contract_kernel, parts, extra, groups, per),
        out_shape=jax.ShapeDtypeStruct((basis, basis), jnp.float32),
        in_specs=[pl.BlockSpec(memory_space=pltpu.SMEM)] + [pl.BlockSpec(memory_space=pl.ANY)] * (2 + len(more)),
        out_specs=pl.BlockSpec(memory_space=pltpu.VMEM),
        scratch_shapes=[
            pltpu.VMEM(tables.shape, jnp.bfloat16),
            pltpu.VMEM(got.shape, jnp.bfloat16),
            pltpu.VMEM((PLANES,) + (more[0].shape if extra else (8, basis)), jnp.bfloat16),
            pltpu.VMEM((count * 16, deep), jnp.bfloat16),
            pltpu.VMEM((count * 8, deep), jnp.bfloat16),
            pltpu.SemaphoreType.DMA((NBLK, 2)),
            pltpu.SemaphoreType.DMA((PLANES,)),
        ],
        compiler_params=pltpu.CompilerParams(vmem_limit_bytes=VMEM),
        name="contract",
    )(me, tables, got, *more)


def swap(rows, mask, count):
    return lax.ppermute(rows, "wide", [(i, i ^ mask) for i in range(count)]) if mask else rows


def widen(rows, bits, count):
    me, size = lax.axis_index("wide"), 2 ** len(bits)
    masks = [sum(bit for place, bit in enumerate(reversed(bits)) if turn >> place & 1) for turn in range(size)]
    got = [swap(rows, mask, count) for mask in masks]
    for place, bit in enumerate(reversed(bits)):
        low = me // bit % 2 == 0
        got = [jnp.where(low, got[turn], got[turn ^ 1 << place]) for turn in range(size)]
    return jnp.stack(got, axis=1).reshape((-1,) + rows.shape[1:])


def choose(pattern, plans):
    def kernel(pattern_ref, out_ref):
        alive = [surplus(pattern_ref, block, 0) for block in range(NBLK)]
        choice = jnp.int32(len(plans) - 1)
        for index, (direct, extra) in reversed(list(enumerate(plans[:-1]))):
            needed = jnp.int32(0)
            for level in range(PLANES):
                pair = jnp.maximum(alive[2 * level] - direct, 0) + jnp.maximum(alive[2 * level + 1] - direct, 0)
                needed = jnp.maximum(needed, pair)
            choice = jnp.where(needed <= extra, index, choice)
        out_ref[0] = choice

    return pl.pallas_call(
        kernel,
        out_shape=jax.ShapeDtypeStruct((1,), jnp.int32),
        in_specs=[pl.BlockSpec(memory_space=pltpu.SMEM)],
        out_specs=pl.BlockSpec(memory_space=pltpu.SMEM),
        name="choose",
    )(pattern)[0]


def share(parts, extra, groups, count, integrals, fitted, occupied, pattern):
    aux, per, basis = integrals.shape
    height = aux // count * per
    plane = count // PLANES
    me = lax.axis_index("wide").astype(jnp.int32).reshape(1)
    packed, *over = pack(
        integrals.reshape(count, height, basis), fitted.reshape(count, height, basis), me, pattern, parts, extra, groups
    )
    panel = occupied[None]
    bits = [1 << place for place in reversed(range(count.bit_length() - 1))]
    doubling = count & (count - 1) == 0
    if doubling:
        panel = widen(panel, bits[:2], count)
    packed, panel, over = lax.optimization_barrier((packed, panel, over))
    got = lax.all_to_all(packed, "wide", split_axis=0, concat_axis=0, tiled=True)
    more = []
    if extra:
        over = [swap(rows, apart, count) for apart, rows in enumerate(over)]
        sorted_rows = sort(jnp.stack(over), me, pattern, sum(parts), extra)
        more = [swap(sorted_rows[away], away * plane, count) for away in range(PLANES)]
    if doubling:
        panel = widen(panel, bits[2:], count)
    else:
        panel = lax.all_gather(panel, "wide", axis=0, tiled=True)
    tables = weights(panel.reshape(basis, -1), pattern, parts, extra)
    return contract(me, got, more, tables, parts, extra, groups, height, per)


def on_device(count, narrow, integrals, fitted, occupied, pattern):
    aux, per, basis = integrals.shape
    groups = next(g for g in (FULL, FULL // 2, 1) if aux // count * per % (16 * g) == 0)
    paired = groups == FULL and count & (count - 1) == 0
    plans = PLANS if paired else [(direct, 0) for direct in range(1, NBLK + 1) if parts_of(direct, groups)]
    branches = [functools.partial(share, parts_of(direct, groups), extra, groups, count) for direct, extra in plans]
    total = lax.switch(choose(pattern, plans), branches, integrals, fitted, occupied, pattern)
    strips = lax.all_to_all(total.reshape(count, per, basis), "wide", split_axis=0, concat_axis=0, tiled=True)
    strip = jnp.sum(strips.reshape(count, per, basis), axis=0)
    return lax.psum(strip, "narrow") if narrow > 1 else strip


def solution(mesh):
    in_specs = (P("narrow", "wide", None), P("narrow", "wide", None), P("wide", None), P())
    out_specs = P("wide", None)
    body = functools.partial(on_device, mesh.shape["wide"], mesh.shape["narrow"])
    return jax.shard_map(body, mesh=mesh, in_specs=in_specs, out_specs=out_specs, check_vma=False)
```

```python
import functools

import jax
import jax.numpy as jnp
import numpy as np
from jax import lax
from jax.experimental import pallas as pl
from jax.experimental.pallas import tpu as pltpu
from jax.sharding import PartitionSpec as P

NBLK = 8
FULL = NBLK // 2
DEPTH = 2048
VMEM = 62 * 2**20
SORT_VMEM = 24 * 2**20
NT = (((1,), (1,)), ((), ()))
PLANES = NBLK // 2
PLANS = ((4, 1), (5, 0), (4, 2), (5, 1), (6, 0), (5, 2), (8, 0))


def parts_of(cap, groups):
    parts = []
    for piece in (FULL, FULL, FULL // 2, FULL // 4):
        if cap >= piece and FULL // piece <= groups:
            parts.append(piece)
            cap -= piece
    return parts if cap == 0 else None


def with_extra(parts, extra):
    return list(parts) + [extra] * (extra > 0)


def lane_layout(parts, extra, basis):
    width = basis // NBLK
    lane = np.arange(basis)
    slot, base, offset = [], [], 0
    for piece in with_extra(parts, extra):
        inner = lane % (basis * piece // FULL)
        slot.append(offset + inner % (piece * width) // width)
        base.append(inner // (piece * width) * basis + inner % width)
        offset += piece
    slot = np.concatenate(slot)
    return np.stack([slot, np.concatenate(base), slot >= sum(parts)]).astype(np.int32)


def surplus(pattern_ref, block, direct):
    alive = jnp.int32(0)
    for other in range(NBLK):
        alive = alive + (pattern_ref[block, other] != 0).astype(jnp.int32)
    return jnp.maximum(alive - direct, 0)


def columns_of(pattern_ref, block, slot, base, width):
    columns = jnp.full(slot.shape, -1, jnp.int32)
    rank = jnp.int32(0)
    for other in range(NBLK):
        alive = pattern_ref[block, other] != 0
        columns = jnp.where(slot == jnp.where(alive, rank, -1), base + other * width, columns)
        rank = rank + alive.astype(jnp.int32)
    return columns


def halves(wide):
    high = wide.astype(jnp.bfloat16)
    return high, (wide - high.astype(jnp.float32)).astype(jnp.bfloat16)


def pack_kernel(parts, extra, groups, me_ref, pattern_ref, layout_ref, ints_hbm, fitted_hbm, *refs):
    out_hbm, over_hbm, (both, out, table, in_sems, out_sems) = refs[0], refs[1:-5], refs[-5:]
    count, rows, lanes = both.shape
    basis = lanes // 2
    chunks = count // PLANES
    step = rows // groups
    direct_rows = out_hbm.shape[1]
    extra_rows = out.shape[1] - direct_rows
    place = lax.rem(me_ref[0], chunks)

    def arrivals(turn):
        here = pl.ds(turn * chunks, chunks)
        return (
            pltpu.make_async_copy(ints_hbm.at[here], both.at[here, :, pl.ds(0, basis)], in_sems.at[turn, 0]),
            pltpu.make_async_copy(fitted_hbm.at[here], both.at[here, :, pl.ds(basis, basis)], in_sems.at[turn, 1]),
        )

    def departures(turn):
        here = pl.ds(turn * chunks, chunks)
        copies = [pltpu.make_async_copy(out.at[here, pl.ds(0, direct_rows)], out_hbm.at[here], out_sems.at[turn, 0])]
        for apart, ref in enumerate(over_hbm):
            source = out.at[turn * chunks + lax.bitwise_xor(place, apart), pl.ds(direct_rows, extra_rows)]
            copies.append(pltpu.make_async_copy(source, ref.at[turn], out_sems.at[turn, 1 + apart]))
        return copies

    for turn in range(PLANES):
        for copy in arrivals(turn):
            copy.start()

    layout = layout_ref[...]
    block = lax.div(me_ref[0] * NBLK, count)
    columns = columns_of(pattern_ref, block, layout[0:1], layout[1:2], basis // NBLK)
    height = lax.broadcasted_iota(jnp.int32, table.shape, 0)
    table[...] = jnp.where(height == columns, 1.0, 0.0).astype(jnp.bfloat16)

    lane = lax.broadcasted_iota(jnp.int32, (chunks * step, basis), 1)

    def work(turn, _):
        for copy in arrivals(turn):
            copy.wait()
        here = pl.ds(turn * chunks, chunks)
        packed = []
        for group in range(groups):
            mine = both[here, pl.ds(group * step, step), :].reshape(chunks * step, lanes)
            packed.append(jnp.dot(mine, table[...], preferred_element_type=jnp.float32))
        start = 0
        for index, piece in enumerate(with_extra(parts, extra)):
            shared = FULL // piece
            held = slice(index * basis, (index + 1) * basis)
            for inner in range(groups // shared):
                total = packed[inner][:, held]
                for other in range(1, shared):
                    theirs = packed[other * (groups // shared) + inner][:, held]
                    total = jnp.where(lane >= other * (basis // shared), theirs, total)
                out[here, pl.ds(start, step), :] = total.astype(jnp.bfloat16).reshape(chunks, step, basis)
                start += step
        for copy in departures(turn):
            copy.start()
        return 0

    lax.fori_loop(0, PLANES, work, 0)
    for turn in range(PLANES):
        for copy in departures(turn):
            copy.wait()


def pack(ints, fitted, me, pattern, parts, extra, groups):
    count, rows, basis = ints.shape
    direct_rows = sum(rows * piece // FULL for piece in parts)
    extra_rows = rows * extra // FULL
    plane = count // PLANES
    layout = lane_layout(parts, extra, basis)
    flops = 2 * count * rows * 2 * basis * layout.shape[1]
    moved = 2 * ints.nbytes + 2 * count * (direct_rows + extra_rows) * basis
    shapes = [jax.ShapeDtypeStruct((count, direct_rows, basis), jnp.bfloat16)]
    if extra:
        shapes += [jax.ShapeDtypeStruct((PLANES, extra_rows, basis), jnp.bfloat16)] * plane
    return pl.pallas_call(
        functools.partial(pack_kernel, parts, extra, groups),
        out_shape=shapes,
        in_specs=[
            pl.BlockSpec(memory_space=pltpu.SMEM),
            pl.BlockSpec(memory_space=pltpu.SMEM),
            pl.BlockSpec(memory_space=pltpu.VMEM),
            pl.BlockSpec(memory_space=pl.ANY),
            pl.BlockSpec(memory_space=pl.ANY),
        ],
        out_specs=[pl.BlockSpec(memory_space=pl.ANY)] * len(shapes),
        scratch_shapes=[
            pltpu.VMEM((count, rows, 2 * basis), jnp.bfloat16),
            pltpu.VMEM((count, direct_rows + extra_rows, basis), jnp.bfloat16),
            pltpu.VMEM((2 * basis, layout.shape[1]), jnp.bfloat16),
            pltpu.SemaphoreType.DMA((PLANES, 2)),
            pltpu.SemaphoreType.DMA((PLANES, len(shapes))),
        ],
        compiler_params=pltpu.CompilerParams(vmem_limit_bytes=VMEM),
        cost_estimate=pl.CostEstimate(flops=flops, bytes_accessed=moved, transcendentals=0),
        name="pack",
    )(me, pattern, jnp.asarray(layout), ints, fitted)


def sort_kernel(direct, me_ref, pattern_ref, slot_ref, over_ref, out_ref):
    planes, sources, _, basis = out_ref.shape
    plane = 2 * sources
    place, level = lax.rem(me_ref[0], plane), lax.div(me_ref[0], plane)
    first = surplus(pattern_ref, 2 * level, direct)
    row = lax.broadcasted_iota(jnp.int32, (basis, basis), 0)
    column = lax.broadcasted_iota(jnp.int32, (basis, basis), 1)
    slot = slot_ref[0:1]
    stay = jnp.where((row == column) & (slot < first), 1.0, 0.0)
    move = jnp.where((row == column - first * (basis // NBLK)) & (slot >= first), 1.0, 0.0)
    table = jnp.concatenate([stay, move], axis=0).astype(jnp.bfloat16)

    def work(away, _):
        there = lax.bitwise_xor(level, away)
        for source in range(sources):
            pair = [over_ref[lax.bitwise_xor(place, second * sources + source), there] for second in range(2)]
            sorted_rows = jnp.dot(jnp.concatenate(pair, axis=1), table, preferred_element_type=jnp.float32)
            out_ref[away, source] = sorted_rows.astype(jnp.bfloat16)
        return 0

    lax.fori_loop(0, planes, work, 0)


def sort(over, me, pattern, direct, extra):
    plane, _, rows, basis = over.shape
    slots = lane_layout((extra,), 0, basis)
    flops = 4 * PLANES * plane // 2 * rows * basis * basis
    return pl.pallas_call(
        functools.partial(sort_kernel, direct),
        out_shape=jax.ShapeDtypeStruct((PLANES, plane // 2, rows, basis), jnp.bfloat16),
        in_specs=[pl.BlockSpec(memory_space=pltpu.SMEM)] * 2 + [pl.BlockSpec(memory_space=pltpu.VMEM)] * 2,
        out_specs=pl.BlockSpec(memory_space=pltpu.VMEM),
        compiler_params=pltpu.CompilerParams(vmem_limit_bytes=SORT_VMEM),
        cost_estimate=pl.CostEstimate(flops=flops, bytes_accessed=2 * over.nbytes, transcendentals=0),
        name="sort",
    )(me, pattern, jnp.asarray(slots), over)


def weights_kernel(direct, pattern_ref, layout_ref, panel_ref, out_ref):
    basis = panel_ref.shape[0]
    lanes = layout_ref.shape[0]
    panel = panel_ref[...]
    gram = lax.dot_general(panel, panel, NT, preferred_element_type=jnp.float32)
    high, low = halves(gram)
    column = lax.broadcasted_iota(jnp.int32, (lanes, 2 * basis), 1)

    def fill(block, _):
        before = lax.rem(block, 2) * surplus(pattern_ref, block - lax.rem(block, 2), direct)
        slot = layout_ref[:, 0:1] - layout_ref[:, 2:3] * before
        slot = jnp.where((layout_ref[:, 2:3] == 0) | (slot >= direct), slot, -2)
        held = columns_of(pattern_ref, block, slot, layout_ref[:, 1:2], basis // NBLK)
        table = jnp.where(column == held, 1.0, 0.0).astype(jnp.bfloat16)
        ints = table[:, :basis]
        out_ref[block, :lanes, :basis] = jnp.dot(ints, high, preferred_element_type=jnp.float32).astype(jnp.bfloat16)
        out_ref[block, :lanes, basis:] = table[:, basis:]
        out_ref[block, lanes:, :basis] = jnp.dot(ints, low, preferred_element_type=jnp.float32).astype(jnp.bfloat16)
        out_ref[block, lanes:, basis:] = jnp.zeros((lanes, basis), jnp.bfloat16)
        return 0

    lax.fori_loop(0, NBLK, fill, 0)


def weights(panel, pattern, parts, extra):
    basis = panel.shape[0]
    layout = lane_layout(parts, extra, basis).T
    lanes = layout.shape[0]
    return pl.pallas_call(
        functools.partial(weights_kernel, sum(parts)),
        out_shape=jax.ShapeDtypeStruct((NBLK, 2 * lanes, 2 * basis), jnp.bfloat16),
        in_specs=[
            pl.BlockSpec(memory_space=pltpu.SMEM),
            pl.BlockSpec(memory_space=pltpu.VMEM),
            pl.BlockSpec(memory_space=pltpu.VMEM),
        ],
        out_specs=pl.BlockSpec(memory_space=pltpu.VMEM),
        compiler_params=pltpu.CompilerParams(vmem_limit_bytes=VMEM),
        cost_estimate=pl.CostEstimate(flops=2 * NBLK * 2 * lanes * basis * basis, bytes_accessed=2 * panel.nbytes, transcendentals=0),
        name="weights",
    )(pattern, jnp.asarray(layout), panel)


def contract_kernel(parts, extra, groups, per, me_ref, tables_hbm, got_hbm, *refs):
    more_hbm = refs[: PLANES if extra else 0]
    out_ref, tables, got, more, left, right, sems, more_sems = refs[len(more_hbm) :]
    count, _, basis = got.shape
    sources = count // NBLK
    height = right.shape[1] // basis * 8
    step = height // groups
    wide = count * 8

    def arrivals(block):
        here = pl.ds(block * sources, sources)
        return (
            pltpu.make_async_copy(tables_hbm.at[block], tables.at[block], sems.at[block, 0]),
            pltpu.make_async_copy(got_hbm.at[here], got.at[here], sems.at[block, 1]),
        )

    def more_arrival(away):
        level = lax.bitwise_xor(lax.div(me_ref[0] * PLANES, count), away)
        return pltpu.make_async_copy(more_hbm[away], more.at[level], more_sems.at[away])

    for block in range(NBLK):
        for copy in arrivals(block):
            copy.start()
        if extra and block == 0:
            for away in range(PLANES):
                more_arrival(away).start()
    for away in range(len(more_hbm)):
        more_arrival(away).wait()

    def unpack(block, _):
        for copy in arrivals(block):
            copy.wait()
        here = pl.ds(block * sources, sources)
        pieces, start = [], 0
        for index, piece in enumerate(with_extra(parts, extra)):
            shared = FULL // piece
            kept = groups // shared * step
            if index < len(parts):
                part = got[here, pl.ds(start, kept), :]
            else:
                part = more[lax.div(block, 2)]
            start += kept
            if shared > 1:
                lane = lax.broadcasted_iota(jnp.int32, part.shape, 2)
                window = basis // shared
                part = jnp.concatenate(
                    [
                        jnp.where((lane >= own * window) & (lane < (own + 1) * window), part, jnp.zeros_like(part))
                        for own in range(shared)
                    ],
                    axis=1,
                )
            pieces.append(part.reshape(sources * height, basis))
        both = jnp.concatenate(pieces + pieces, axis=1)
        turned = jnp.dot(both, tables[block], preferred_element_type=jnp.float32).reshape(sources, height, 2 * basis)
        rows = pl.ds(pl.multiple_of(block * (sources * 8), sources * 8), sources * 8)
        low_rows = pl.ds(pl.multiple_of(block * (sources * 8) + wide, sources * 8), sources * 8)
        for eight in range(height // 8):
            lanes = slice(eight * basis, (eight + 1) * basis)
            mine = turned[:, eight * 8 : eight * 8 + 8, :].reshape(sources * 8, 2 * basis)
            high = mine[:, :basis].astype(jnp.bfloat16)
            left[rows, lanes] = high
            left[low_rows, lanes] = (mine[:, :basis] - high.astype(jnp.float32)).astype(jnp.bfloat16)
            right[rows, lanes] = mine[:, basis:].astype(jnp.bfloat16)
        return 0

    lax.fori_loop(0, NBLK, unpack, 0)
    turns = right.shape[1] // DEPTH if right.shape[1] % DEPTH == 0 else 1
    depth = right.shape[1] // turns

    def multiply(turn, sums):
        lanes = pl.ds(pl.multiple_of(turn * depth, depth), depth)
        return sums + lax.dot_general(left[:, lanes], right[:, lanes], NT, preferred_element_type=jnp.float32)

    total = lax.fori_loop(0, turns, multiply, jnp.zeros((2 * wide, wide), jnp.float32))
    total = total[:wide] + total[wide:]
    row = lax.broadcasted_iota(jnp.int32, (wide, wide), 0) % 8 // per
    column = lax.broadcasted_iota(jnp.int32, (wide, wide), 1) % 8 // per
    total = jnp.where(row == column, total, 0.0)
    spot = lax.broadcasted_iota(jnp.int32, (basis, wide), 1)
    spot = spot // 8 * per + spot % per
    fold = jnp.where(spot == lax.broadcasted_iota(jnp.int32, (basis, wide), 0), 1.0, 0.0).astype(jnp.bfloat16)
    high, low = halves(total)
    total = jnp.dot(fold, high, preferred_element_type=jnp.float32) + jnp.dot(
        fold, low, preferred_element_type=jnp.float32
    )
    high, low = halves(total)
    total = lax.dot_general(high, fold, NT, preferred_element_type=jnp.float32) + lax.dot_general(
        low, fold, NT, preferred_element_type=jnp.float32
    )
    out_ref[...] = total + total.T


def contract(me, got, more, tables, parts, extra, groups, height, per):
    count, _, basis = got.shape
    deep = height // 8 * basis
    return pl.pallas_call(
        functools.partial(contract_kernel, parts, extra, groups, per),
        out_shape=jax.ShapeDtypeStruct((basis, basis), jnp.float32),
        in_specs=[pl.BlockSpec(memory_space=pltpu.SMEM)] + [pl.BlockSpec(memory_space=pl.ANY)] * (2 + len(more)),
        out_specs=pl.BlockSpec(memory_space=pltpu.VMEM),
        scratch_shapes=[
            pltpu.VMEM(tables.shape, jnp.bfloat16),
            pltpu.VMEM(got.shape, jnp.bfloat16),
            pltpu.VMEM((PLANES,) + (more[0].shape if extra else (8, basis)), jnp.bfloat16),
            pltpu.VMEM((count * 16, deep), jnp.bfloat16),
            pltpu.VMEM((count * 8, deep), jnp.bfloat16),
            pltpu.SemaphoreType.DMA((NBLK, 2)),
            pltpu.SemaphoreType.DMA((PLANES,)),
        ],
        compiler_params=pltpu.CompilerParams(vmem_limit_bytes=VMEM),
        name="contract",
    )(me, tables, got, *more)


def swap(rows, mask, count):
    return lax.ppermute(rows, "wide", [(i, i ^ mask) for i in range(count)]) if mask else rows


def widen(rows, bits, count):
    me, size = lax.axis_index("wide"), 2 ** len(bits)
    masks = [sum(bit for place, bit in enumerate(reversed(bits)) if turn >> place & 1) for turn in range(size)]
    got = [swap(rows, mask, count) for mask in masks]
    for place, bit in enumerate(reversed(bits)):
        low = me // bit % 2 == 0
        got = [jnp.where(low, got[turn], got[turn ^ 1 << place]) for turn in range(size)]
    return jnp.stack(got, axis=1).reshape((-1,) + rows.shape[1:])


def choose(pattern, plans):
    def kernel(pattern_ref, out_ref):
        alive = [surplus(pattern_ref, block, 0) for block in range(NBLK)]
        choice = jnp.int32(len(plans) - 1)
        for index, (direct, extra) in reversed(list(enumerate(plans[:-1]))):
            needed = jnp.int32(0)
            for level in range(PLANES):
                pair = jnp.maximum(alive[2 * level] - direct, 0) + jnp.maximum(alive[2 * level + 1] - direct, 0)
                needed = jnp.maximum(needed, pair)
            choice = jnp.where(needed <= extra, index, choice)
        out_ref[0] = choice

    return pl.pallas_call(
        kernel,
        out_shape=jax.ShapeDtypeStruct((1,), jnp.int32),
        in_specs=[pl.BlockSpec(memory_space=pltpu.SMEM)],
        out_specs=pl.BlockSpec(memory_space=pltpu.SMEM),
        name="choose",
    )(pattern)[0]


def share(parts, extra, groups, count, integrals, fitted, occupied, pattern):
    aux, per, basis = integrals.shape
    height = aux // count * per
    plane = count // PLANES
    me = lax.axis_index("wide").astype(jnp.int32).reshape(1)
    packed, *over = pack(
        integrals.reshape(count, height, basis), fitted.reshape(count, height, basis), me, pattern, parts, extra, groups
    )
    panel = occupied[None]
    bits = [1 << place for place in reversed(range(count.bit_length() - 1))]
    doubling = count & (count - 1) == 0
    if doubling:
        panel = widen(panel, bits[:2], count)
    packed, panel, over = lax.optimization_barrier((packed, panel, over))
    got = lax.all_to_all(packed, "wide", split_axis=0, concat_axis=0, tiled=True)
    more = []
    if extra:
        over = [swap(rows, apart, count) for apart, rows in enumerate(over)]
        sorted_rows = sort(jnp.stack(over), me, pattern, sum(parts), extra)
        more = [swap(sorted_rows[away], away * plane, count) for away in range(PLANES)]
    if doubling:
        panel = widen(panel, bits[2:], count)
    else:
        panel = lax.all_gather(panel, "wide", axis=0, tiled=True)
    tables = weights(panel.reshape(basis, -1), pattern, parts, extra)
    return contract(me, got, more, tables, parts, extra, groups, height, per)


def on_device(count, narrow, integrals, fitted, occupied, pattern):
    aux, per, basis = integrals.shape
    groups = next(g for g in (FULL, FULL // 2, 1) if aux // count * per % (16 * g) == 0)
    paired = groups == FULL and count & (count - 1) == 0
    plans = PLANS if paired else [(direct, 0) for direct in range(1, NBLK + 1) if parts_of(direct, groups)]
    branches = [functools.partial(share, parts_of(direct, groups), extra, groups, count) for direct, extra in plans]
    total = lax.switch(choose(pattern, plans), branches, integrals, fitted, occupied, pattern)
    strips = lax.all_to_all(total.reshape(count, per, basis), "wide", split_axis=0, concat_axis=0, tiled=True)
    strip = jnp.sum(strips.reshape(count, per, basis), axis=0)
    return lax.psum(strip, "narrow") if narrow > 1 else strip


def solution(mesh):
    in_specs = (P("narrow", "wide", None), P("narrow", "wide", None), P("wide", None), P())
    out_specs = P("wide", None)
    body = functools.partial(on_device, mesh.shape["wide"], mesh.shape["narrow"])
    return jax.shard_map(body, mesh=mesh, in_specs=in_specs, out_specs=out_specs, check_vma=False)
```

```python
import functools

import jax
import jax.numpy as jnp
import numpy as np
from jax import lax
from jax.experimental import pallas as pl
from jax.experimental.pallas import tpu as pltpu
from jax.sharding import PartitionSpec as P

NBLK = 8
FULL = NBLK // 2
DEPTH = 2048
VMEM = 62 * 2**20
SORT_VMEM = 24 * 2**20
NT = (((1,), (1,)), ((), ()))
PLANES = NBLK // 2
PLANS = ((4, 1), (5, 0), (4, 2), (6, 0), (5, 2), (8, 0))


def parts_of(cap, groups):
    parts = []
    for piece in (FULL, FULL, FULL // 2, FULL // 4):
        if cap >= piece and FULL // piece <= groups:
            parts.append(piece)
            cap -= piece
    return parts if cap == 0 else None


def with_extra(parts, extra):
    return list(parts) + [extra] * (extra > 0)


def lane_layout(parts, extra, basis):
    width = basis // NBLK
    lane = np.arange(basis)
    slot, base, offset = [], [], 0
    for piece in with_extra(parts, extra):
        inner = lane % (basis * piece // FULL)
        slot.append(offset + inner % (piece * width) // width)
        base.append(inner // (piece * width) * basis + inner % width)
        offset += piece
    slot = np.concatenate(slot)
    return np.stack([slot, np.concatenate(base), slot >= sum(parts)]).astype(np.int32)


def surplus(pattern_ref, block, direct):
    alive = jnp.int32(0)
    for other in range(NBLK):
        alive = alive + (pattern_ref[block, other] != 0).astype(jnp.int32)
    return jnp.maximum(alive - direct, 0)


def columns_of(pattern_ref, block, slot, base, width):
    columns = jnp.full(slot.shape, -1, jnp.int32)
    rank = jnp.int32(0)
    for other in range(NBLK):
        alive = pattern_ref[block, other] != 0
        columns = jnp.where(slot == jnp.where(alive, rank, -1), base + other * width, columns)
        rank = rank + alive.astype(jnp.int32)
    return columns


def halves(wide):
    high = wide.astype(jnp.bfloat16)
    return high, (wide - high.astype(jnp.float32)).astype(jnp.bfloat16)


def pack_kernel(parts, extra, groups, me_ref, pattern_ref, layout_ref, ints_hbm, fitted_hbm, *refs):
    out_hbm, over_hbm, (both, out, table, in_sems, out_sems) = refs[0], refs[1:-5], refs[-5:]
    count, rows, lanes = both.shape
    basis = lanes // 2
    chunks = count // PLANES
    step = rows // groups
    direct_rows = out_hbm.shape[1]
    extra_rows = out.shape[1] - direct_rows
    place = lax.rem(me_ref[0], chunks)

    def arrivals(turn):
        here = pl.ds(turn * chunks, chunks)
        return (
            pltpu.make_async_copy(ints_hbm.at[here], both.at[here, :, pl.ds(0, basis)], in_sems.at[turn, 0]),
            pltpu.make_async_copy(fitted_hbm.at[here], both.at[here, :, pl.ds(basis, basis)], in_sems.at[turn, 1]),
        )

    def departures(turn):
        here = pl.ds(turn * chunks, chunks)
        copies = [pltpu.make_async_copy(out.at[here, pl.ds(0, direct_rows)], out_hbm.at[here], out_sems.at[turn, 0])]
        for apart, ref in enumerate(over_hbm):
            source = out.at[turn * chunks + lax.bitwise_xor(place, apart), pl.ds(direct_rows, extra_rows)]
            copies.append(pltpu.make_async_copy(source, ref.at[turn], out_sems.at[turn, 1 + apart]))
        return copies

    for turn in range(PLANES):
        for copy in arrivals(turn):
            copy.start()

    layout = layout_ref[...]
    block = lax.div(me_ref[0] * NBLK, count)
    columns = columns_of(pattern_ref, block, layout[0:1], layout[1:2], basis // NBLK)
    height = lax.broadcasted_iota(jnp.int32, table.shape, 0)
    table[...] = jnp.where(height == columns, 1.0, 0.0).astype(jnp.bfloat16)

    lane = lax.broadcasted_iota(jnp.int32, (chunks * step, basis), 1)

    def work(turn, _):
        for copy in arrivals(turn):
            copy.wait()
        here = pl.ds(turn * chunks, chunks)
        packed = []
        for group in range(groups):
            mine = both[here, pl.ds(group * step, step), :].reshape(chunks * step, lanes)
            packed.append(jnp.dot(mine, table[...], preferred_element_type=jnp.float32))
        start = 0
        for index, piece in enumerate(with_extra(parts, extra)):
            shared = FULL // piece
            held = slice(index * basis, (index + 1) * basis)
            for inner in range(groups // shared):
                total = packed[inner][:, held]
                for other in range(1, shared):
                    theirs = packed[other * (groups // shared) + inner][:, held]
                    total = jnp.where(lane >= other * (basis // shared), theirs, total)
                out[here, pl.ds(start, step), :] = total.astype(jnp.bfloat16).reshape(chunks, step, basis)
                start += step
        for copy in departures(turn):
            copy.start()
        return 0

    lax.fori_loop(0, PLANES, work, 0)
    for turn in range(PLANES):
        for copy in departures(turn):
            copy.wait()


def pack(ints, fitted, me, pattern, parts, extra, groups):
    count, rows, basis = ints.shape
    direct_rows = sum(rows * piece // FULL for piece in parts)
    extra_rows = rows * extra // FULL
    plane = count // PLANES
    layout = lane_layout(parts, extra, basis)
    flops = 2 * count * rows * 2 * basis * layout.shape[1]
    moved = 2 * ints.nbytes + 2 * count * (direct_rows + extra_rows) * basis
    shapes = [jax.ShapeDtypeStruct((count, direct_rows, basis), jnp.bfloat16)]
    if extra:
        shapes += [jax.ShapeDtypeStruct((PLANES, extra_rows, basis), jnp.bfloat16)] * plane
    return pl.pallas_call(
        functools.partial(pack_kernel, parts, extra, groups),
        out_shape=shapes,
        in_specs=[
            pl.BlockSpec(memory_space=pltpu.SMEM),
            pl.BlockSpec(memory_space=pltpu.SMEM),
            pl.BlockSpec(memory_space=pltpu.VMEM),
            pl.BlockSpec(memory_space=pl.ANY),
            pl.BlockSpec(memory_space=pl.ANY),
        ],
        out_specs=[pl.BlockSpec(memory_space=pl.ANY)] * len(shapes),
        scratch_shapes=[
            pltpu.VMEM((count, rows, 2 * basis), jnp.bfloat16),
            pltpu.VMEM((count, direct_rows + extra_rows, basis), jnp.bfloat16),
            pltpu.VMEM((2 * basis, layout.shape[1]), jnp.bfloat16),
            pltpu.SemaphoreType.DMA((PLANES, 2)),
            pltpu.SemaphoreType.DMA((PLANES, len(shapes))),
        ],
        compiler_params=pltpu.CompilerParams(vmem_limit_bytes=VMEM),
        cost_estimate=pl.CostEstimate(flops=flops, bytes_accessed=moved, transcendentals=0),
        name="pack",
    )(me, pattern, jnp.asarray(layout), ints, fitted)


def sort_kernel(direct, me_ref, pattern_ref, slot_ref, over_ref, out_ref):
    planes, sources, _, basis = out_ref.shape
    plane = 2 * sources
    place, level = lax.rem(me_ref[0], plane), lax.div(me_ref[0], plane)
    first = surplus(pattern_ref, 2 * level, direct)
    row = lax.broadcasted_iota(jnp.int32, (basis, basis), 0)
    column = lax.broadcasted_iota(jnp.int32, (basis, basis), 1)
    slot = slot_ref[0:1]
    stay = jnp.where((row == column) & (slot < first), 1.0, 0.0)
    move = jnp.where((row == column - first * (basis // NBLK)) & (slot >= first), 1.0, 0.0)
    table = jnp.concatenate([stay, move], axis=0).astype(jnp.bfloat16)

    def work(away, _):
        there = lax.bitwise_xor(level, away)
        for source in range(sources):
            pair = [over_ref[lax.bitwise_xor(place, second * sources + source), there] for second in range(2)]
            sorted_rows = jnp.dot(jnp.concatenate(pair, axis=1), table, preferred_element_type=jnp.float32)
            out_ref[away, source] = sorted_rows.astype(jnp.bfloat16)
        return 0

    lax.fori_loop(0, planes, work, 0)


def sort(over, me, pattern, direct, extra):
    plane, _, rows, basis = over.shape
    slots = lane_layout((extra,), 0, basis)
    flops = 4 * PLANES * plane // 2 * rows * basis * basis
    return pl.pallas_call(
        functools.partial(sort_kernel, direct),
        out_shape=jax.ShapeDtypeStruct((PLANES, plane // 2, rows, basis), jnp.bfloat16),
        in_specs=[pl.BlockSpec(memory_space=pltpu.SMEM)] * 2 + [pl.BlockSpec(memory_space=pltpu.VMEM)] * 2,
        out_specs=pl.BlockSpec(memory_space=pltpu.VMEM),
        compiler_params=pltpu.CompilerParams(vmem_limit_bytes=SORT_VMEM),
        cost_estimate=pl.CostEstimate(flops=flops, bytes_accessed=2 * over.nbytes, transcendentals=0),
        name="sort",
    )(me, pattern, jnp.asarray(slots), over)


def weights_kernel(direct, pattern_ref, layout_ref, panel_ref, out_ref):
    basis = panel_ref.shape[0]
    lanes = layout_ref.shape[0]
    panel = panel_ref[...]
    gram = lax.dot_general(panel, panel, NT, preferred_element_type=jnp.float32)
    high, low = halves(gram)
    column = lax.broadcasted_iota(jnp.int32, (lanes, 2 * basis), 1)

    def fill(block, _):
        before = lax.rem(block, 2) * surplus(pattern_ref, block - lax.rem(block, 2), direct)
        slot = layout_ref[:, 0:1] - layout_ref[:, 2:3] * before
        slot = jnp.where((layout_ref[:, 2:3] == 0) | (slot >= direct), slot, -2)
        held = columns_of(pattern_ref, block, slot, layout_ref[:, 1:2], basis // NBLK)
        table = jnp.where(column == held, 1.0, 0.0).astype(jnp.bfloat16)
        ints = table[:, :basis]
        out_ref[block, :lanes, :basis] = jnp.dot(ints, high, preferred_element_type=jnp.float32).astype(jnp.bfloat16)
        out_ref[block, :lanes, basis:] = table[:, basis:]
        out_ref[block, lanes:, :basis] = jnp.dot(ints, low, preferred_element_type=jnp.float32).astype(jnp.bfloat16)
        out_ref[block, lanes:, basis:] = jnp.zeros((lanes, basis), jnp.bfloat16)
        return 0

    lax.fori_loop(0, NBLK, fill, 0)


def weights(panel, pattern, parts, extra):
    basis = panel.shape[0]
    layout = lane_layout(parts, extra, basis).T
    lanes = layout.shape[0]
    return pl.pallas_call(
        functools.partial(weights_kernel, sum(parts)),
        out_shape=jax.ShapeDtypeStruct((NBLK, 2 * lanes, 2 * basis), jnp.bfloat16),
        in_specs=[
            pl.BlockSpec(memory_space=pltpu.SMEM),
            pl.BlockSpec(memory_space=pltpu.VMEM),
            pl.BlockSpec(memory_space=pltpu.VMEM),
        ],
        out_specs=pl.BlockSpec(memory_space=pltpu.VMEM),
        compiler_params=pltpu.CompilerParams(vmem_limit_bytes=VMEM),
        cost_estimate=pl.CostEstimate(flops=2 * NBLK * 2 * lanes * basis * basis, bytes_accessed=2 * panel.nbytes, transcendentals=0),
        name="weights",
    )(pattern, jnp.asarray(layout), panel)


def contract_kernel(parts, extra, groups, per, me_ref, tables_hbm, got_hbm, *refs):
    more_hbm = refs[: PLANES if extra else 0]
    out_ref, tables, got, more, left, right, sems, more_sems = refs[len(more_hbm) :]
    count, _, basis = got.shape
    sources = count // NBLK
    height = right.shape[1] // basis * 8
    step = height // groups
    wide = count * 8

    def arrivals(block):
        here = pl.ds(block * sources, sources)
        return (
            pltpu.make_async_copy(tables_hbm.at[block], tables.at[block], sems.at[block, 0]),
            pltpu.make_async_copy(got_hbm.at[here], got.at[here], sems.at[block, 1]),
        )

    def more_arrival(away):
        level = lax.bitwise_xor(lax.div(me_ref[0] * PLANES, count), away)
        return pltpu.make_async_copy(more_hbm[away], more.at[level], more_sems.at[away])

    for block in range(NBLK):
        for copy in arrivals(block):
            copy.start()
        if extra and block == 0:
            for away in range(PLANES):
                more_arrival(away).start()
    for away in range(len(more_hbm)):
        more_arrival(away).wait()

    def unpack(block, _):
        for copy in arrivals(block):
            copy.wait()
        here = pl.ds(block * sources, sources)
        pieces, start = [], 0
        for index, piece in enumerate(with_extra(parts, extra)):
            shared = FULL // piece
            kept = groups // shared * step
            if index < len(parts):
                part = got[here, pl.ds(start, kept), :]
            else:
                part = more[lax.div(block, 2)]
            start += kept
            if shared > 1:
                lane = lax.broadcasted_iota(jnp.int32, part.shape, 2)
                window = basis // shared
                part = jnp.concatenate(
                    [
                        jnp.where((lane >= own * window) & (lane < (own + 1) * window), part, jnp.zeros_like(part))
                        for own in range(shared)
                    ],
                    axis=1,
                )
            pieces.append(part.reshape(sources * height, basis))
        both = jnp.concatenate(pieces + pieces, axis=1)
        turned = jnp.dot(both, tables[block], preferred_element_type=jnp.float32).reshape(sources, height, 2 * basis)
        rows = pl.ds(pl.multiple_of(block * (sources * 8), sources * 8), sources * 8)
        low_rows = pl.ds(pl.multiple_of(block * (sources * 8) + wide, sources * 8), sources * 8)
        for eight in range(height // 8):
            lanes = slice(eight * basis, (eight + 1) * basis)
            mine = turned[:, eight * 8 : eight * 8 + 8, :].reshape(sources * 8, 2 * basis)
            high = mine[:, :basis].astype(jnp.bfloat16)
            left[rows, lanes] = high
            left[low_rows, lanes] = (mine[:, :basis] - high.astype(jnp.float32)).astype(jnp.bfloat16)
            right[rows, lanes] = mine[:, basis:].astype(jnp.bfloat16)
        return 0

    lax.fori_loop(0, NBLK, unpack, 0)
    turns = right.shape[1] // DEPTH if right.shape[1] % DEPTH == 0 else 1
    depth = right.shape[1] // turns

    def multiply(turn, sums):
        lanes = pl.ds(pl.multiple_of(turn * depth, depth), depth)
        return sums + lax.dot_general(left[:, lanes], right[:, lanes], NT, preferred_element_type=jnp.float32)

    total = lax.fori_loop(0, turns, multiply, jnp.zeros((2 * wide, wide), jnp.float32))
    total = total[:wide] + total[wide:]
    row = lax.broadcasted_iota(jnp.int32, (wide, wide), 0) % 8 // per
    column = lax.broadcasted_iota(jnp.int32, (wide, wide), 1) % 8 // per
    total = jnp.where(row == column, total, 0.0)
    spot = lax.broadcasted_iota(jnp.int32, (basis, wide), 1)
    spot = spot // 8 * per + spot % per
    fold = jnp.where(spot == lax.broadcasted_iota(jnp.int32, (basis, wide), 0), 1.0, 0.0).astype(jnp.bfloat16)
    high, low = halves(total)
    total = jnp.dot(fold, high, preferred_element_type=jnp.float32) + jnp.dot(
        fold, low, preferred_element_type=jnp.float32
    )
    high, low = halves(total)
    total = lax.dot_general(high, fold, NT, preferred_element_type=jnp.float32) + lax.dot_general(
        low, fold, NT, preferred_element_type=jnp.float32
    )
    out_ref[...] = total + total.T


def contract(me, got, more, tables, parts, extra, groups, height, per):
    count, _, basis = got.shape
    deep = height // 8 * basis
    return pl.pallas_call(
        functools.partial(contract_kernel, parts, extra, groups, per),
        out_shape=jax.ShapeDtypeStruct((basis, basis), jnp.float32),
        in_specs=[pl.BlockSpec(memory_space=pltpu.SMEM)] + [pl.BlockSpec(memory_space=pl.ANY)] * (2 + len(more)),
        out_specs=pl.BlockSpec(memory_space=pltpu.VMEM),
        scratch_shapes=[
            pltpu.VMEM(tables.shape, jnp.bfloat16),
            pltpu.VMEM(got.shape, jnp.bfloat16),
            pltpu.VMEM((PLANES,) + (more[0].shape if extra else (8, basis)), jnp.bfloat16),
            pltpu.VMEM((count * 16, deep), jnp.bfloat16),
            pltpu.VMEM((count * 8, deep), jnp.bfloat16),
            pltpu.SemaphoreType.DMA((NBLK, 2)),
            pltpu.SemaphoreType.DMA((PLANES,)),
        ],
        compiler_params=pltpu.CompilerParams(vmem_limit_bytes=VMEM),
        name="contract",
    )(me, tables, got, *more)


def swap(rows, mask, count):
    return lax.ppermute(rows, "wide", [(i, i ^ mask) for i in range(count)]) if mask else rows


def widen(rows, bits, count):
    me, size = lax.axis_index("wide"), 2 ** len(bits)
    masks = [sum(bit for place, bit in enumerate(reversed(bits)) if turn >> place & 1) for turn in range(size)]
    got = [swap(rows, mask, count) for mask in masks]
    for place, bit in enumerate(reversed(bits)):
        low = me // bit % 2 == 0
        got = [jnp.where(low, got[turn], got[turn ^ 1 << place]) for turn in range(size)]
    return jnp.stack(got, axis=1).reshape((-1,) + rows.shape[1:])


def choose(pattern, plans):
    def kernel(pattern_ref, out_ref):
        alive = [surplus(pattern_ref, block, 0) for block in range(NBLK)]
        choice = jnp.int32(len(plans) - 1)
        for index, (direct, extra) in reversed(list(enumerate(plans[:-1]))):
            needed = jnp.int32(0)
            for level in range(PLANES):
                pair = jnp.maximum(alive[2 * level] - direct, 0) + jnp.maximum(alive[2 * level + 1] - direct, 0)
                needed = jnp.maximum(needed, pair)
            choice = jnp.where(needed <= extra, index, choice)
        out_ref[0] = choice

    return pl.pallas_call(
        kernel,
        out_shape=jax.ShapeDtypeStruct((1,), jnp.int32),
        in_specs=[pl.BlockSpec(memory_space=pltpu.SMEM)],
        out_specs=pl.BlockSpec(memory_space=pltpu.SMEM),
        name="choose",
    )(pattern)[0]


def share(parts, extra, groups, count, integrals, fitted, occupied, pattern):
    aux, per, basis = integrals.shape
    height = aux // count * per
    plane = count // PLANES
    me = lax.axis_index("wide").astype(jnp.int32).reshape(1)
    packed, *over = pack(
        integrals.reshape(count, height, basis), fitted.reshape(count, height, basis), me, pattern, parts, extra, groups
    )
    panel = occupied[None]
    bits = [1 << place for place in reversed(range(count.bit_length() - 1))]
    doubling = count & (count - 1) == 0
    if doubling:
        panel = widen(panel, bits[:2], count)
    packed, panel, over = lax.optimization_barrier((packed, panel, over))
    got = lax.all_to_all(packed, "wide", split_axis=0, concat_axis=0, tiled=True)
    more = []
    if extra:
        over = [swap(rows, apart, count) for apart, rows in enumerate(over)]
        sorted_rows = sort(jnp.stack(over), me, pattern, sum(parts), extra)
        more = [swap(sorted_rows[away], away * plane, count) for away in range(PLANES)]
    if doubling:
        panel = widen(panel, bits[2:], count)
    else:
        panel = lax.all_gather(panel, "wide", axis=0, tiled=True)
    tables = weights(panel.reshape(basis, -1), pattern, parts, extra)
    return contract(me, got, more, tables, parts, extra, groups, height, per)


def on_device(count, narrow, integrals, fitted, occupied, pattern):
    aux, per, basis = integrals.shape
    groups = next(g for g in (FULL, FULL // 2, 1) if aux // count * per % (16 * g) == 0)
    paired = groups == FULL and count & (count - 1) == 0
    plans = PLANS if paired else [(direct, 0) for direct in range(1, NBLK + 1) if parts_of(direct, groups)]
    branches = [functools.partial(share, parts_of(direct, groups), extra, groups, count) for direct, extra in plans]
    total = lax.switch(choose(pattern, plans), branches, integrals, fitted, occupied, pattern)
    strips = lax.all_to_all(total.reshape(count, per, basis), "wide", split_axis=0, concat_axis=0, tiled=True)
    strip = jnp.sum(strips.reshape(count, per, basis), axis=0)
    return lax.psum(strip, "narrow") if narrow > 1 else strip


def solution(mesh):
    in_specs = (P("narrow", "wide", None), P("narrow", "wide", None), P("wide", None), P())
    out_specs = P("wide", None)
    body = functools.partial(on_device, mesh.shape["wide"], mesh.shape["narrow"])
    return jax.shard_map(body, mesh=mesh, in_specs=in_specs, out_specs=out_specs, check_vma=False)
```
